128 devices in a mesh: dp: 16 (over x, z), tensor: 8 (over y, core).
Axes of the slice: x: 4, y: 4, z: 4, core: 2. Of those that a mesh axis runs over, the one named last changes fastest.
Arguments:
- frames: bfloat16 [4096, 1536], P('dp', 'tensor'), may hold values from -6 to 6
- counts: int32 [16], P('dp'), may hold values from 1 to 256, as said below
- layer_norm_gain1: float32 [1536], replicated, may hold values from 0.1 to 1.9
- w_in: bfloat16 [1536, 4096], P('dp', 'tensor'), may hold values from -0.15625 to 0.15625
- w_out: bfloat16 [4096, 1536], P('tensor', 'dp'), may hold values from -0.09375 to 0.09375
- norm_gain2: float32 [1536], replicated, may hold values from 0.1 to 1.9
- w_adapt: bfloat16 [1536, 8192], P('dp', 'tensor'), may hold values from -0.15625 to 0.15625
- grad_out: bfloat16 [4096, 8192], P('dp', 'tensor'), may hold values from -0.1796875 to 0.1796875
Outputs:
- adapted: bfloat16 [4096, 8192], P('dp', 'tensor')
- frames_gradient: float32 [4096, 1536], P('dp', 'tensor')
- grad_in: float32 [1536, 4096], P('dp', 'tensor')
- grad_outw: float32 [4096, 1536], P('tensor', 'dp')
- grad_adapt: float32 [1536, 8192], P('dp', 'tensor')
- gain1_gradient: float32 [1536], replicated
- grad_gain2: float32 [1536], replicated
The draws below stay inside these ranges and needn't reach their ends.
Inputs may be any that keep to these rules, and one draw needn't show every extreme that they name: `counts`: each utterance has 1 to 256 live frames; some utterance has all 256. Indices of dp differ in their typical lengths by up to four times.
All inputs are finite; a program needn't handle non-finite values.
Results may differ from the reference program's by a relative error of at most 0.006.
Values may be sent and summed in bfloat16 or wider, within the bound.
A program may use at most 128 MiB of HBM per device.

```python
import jax
import jax.numpy as jnp
from jax import lax

D = 1536
FF = 4096
DA = 8192
SPAN = 256
U_DEV = 1
UTTS = 16
FRAMES = 4096


def draw_counts(key, part):
    key = jax.random.fold_in(key, 7)
    key_level, key_raw = jax.random.split(key)
    ranks = UTTS // U_DEV
    level = jax.random.randint(key_level, (ranks, 1), 1, 5)
    raw_draw = jax.random.randint(key_raw, (ranks, U_DEV), 0, 1 << 20)
    upper = jnp.maximum(level * SPAN // 4, 1)
    result = 1 + raw_draw % upper
    result = result.at[0, 0].set(SPAN)
    return result.reshape(-1).astype(jnp.int32)


def block_levels(key, dims, shards, smallest, high):
    factor_of = 1.0
    for axis_at, shards_of in shards:
        heights = jax.random.uniform(jax.random.fold_in(jax.random.fold_in(key, 6), axis_at), (shards_of,), jnp.float32, smallest / len(shards), high / len(shards))
        factor_of = factor_of * jnp.repeat(jnp.exp(heights), dims[axis_at] // shards_of).reshape((-1,) + (1,) * (len(dims) - 1 - axis_at))
    return factor_of


def centred(stream_key, shape, width, bound, cuts=(), held_as=jnp.bfloat16):
    factor_of = block_levels(stream_key, shape, cuts, -0.22, 0.18) if cuts else 1.0
    drawn = jax.random.normal(stream_key, shape, jnp.float32) * width * factor_of
    return jnp.minimum(jnp.maximum(drawn, -bound), bound).astype(held_as)


def setup_inputs(seed: int = 0) -> dict:
    arg_keys = jax.random.split(jax.random.key(seed), 9)
    return {
        "frames": centred(arg_keys[0], (FRAMES, D), 1.0, 6.0, ((0, 16), (1, 8))),
        "counts": draw_counts(jax.random.fold_in(arg_keys[8], 71), 0),
        "layer_norm_gain1": jnp.clip(1.0 + 0.18 * jax.random.normal(arg_keys[2], (D,), jnp.float32), 0.1, 1.9),
        "w_in": centred(arg_keys[3], (D, FF), D ** -0.5, 0.15625, ((0, 16), (1, 8))),
        "w_out": centred(arg_keys[4], (FF, D), FF ** -0.5, 0.09375, ((0, 8), (1, 16))),
        "norm_gain2": jnp.clip(1.0 + 0.18 * jax.random.normal(arg_keys[5], (D,), jnp.float32), 0.1, 1.9),
        "w_adapt": centred(arg_keys[6], (D, DA), D ** -0.5, 0.15625, ((0, 16), (1, 8))),
        "grad_out": centred(arg_keys[7], (FRAMES, DA), 0.03, 0.1796875, ((0, 16), (1, 8))),
    }


EPS = 1e-05

def apply_layer_norm(values):
    center = values - lax.optimization_barrier(jnp.mean(values, axis=-1, keepdims=True))
    scale = lax.rsqrt(lax.optimization_barrier(jnp.mean(center * center, axis=-1, keepdims=True)) + EPS)
    return (center * scale, scale)

def norm_input_gradient(d_hat, vhat, scale):
    first = lax.optimization_barrier(jnp.mean(d_hat, axis=-1, keepdims=True))
    second = lax.optimization_barrier(jnp.mean(d_hat * vhat, axis=-1, keepdims=True))
    return scale * (d_hat - first - vhat * second)

def contract(left, right, left_dim, right_dim):
    return lax.dot_general(left, right, (((left_dim,), (right_dim,)), ((), ())), preferred_element_type=jnp.float32)

def reference(frames, counts, layer_norm_gain1, w_in, w_out, norm_gain2, w_adapt, grad_out):
    live = jnp.arange(SPAN, dtype=jnp.int32)[None, :] < counts[:, None]
    live_mask = live.reshape(-1).astype(jnp.bfloat16)[:, None]
    frame_float = frames.astype(jnp.float32)
    normalized_input, inverse_deviation1 = apply_layer_norm(frame_float)
    hidden_activation = (normalized_input * layer_norm_gain1).astype(jnp.bfloat16)
    pre_act = jnp.dot(hidden_activation, w_in, preferred_element_type=jnp.float32)
    sig = jax.nn.sigmoid(pre_act)
    swished = (pre_act * sig).astype(jnp.bfloat16)
    branch = jnp.dot(swished, w_out, preferred_element_type=jnp.float32)
    resid = frame_float + 0.5 * branch
    yhat, rstd2 = apply_layer_norm(resid)
    normed = (yhat * norm_gain2).astype(jnp.bfloat16)
    projected = jnp.dot(normed, w_adapt, preferred_element_type=jnp.float32)
    adapted = (projected * live_mask.astype(jnp.float32)).astype(jnp.bfloat16)
    cot = grad_out * live_mask
    d_normed = contract(cot, w_adapt, 1, 1)
    grad_adapt = contract(normed, cot, 0, 0)
    grad_gain2 = lax.optimization_barrier(jnp.sum(d_normed * yhat, axis=0))
    residual_gradient = norm_input_gradient(d_normed * norm_gain2, yhat, rstd2)
    d_branch = (0.5 * residual_gradient).astype(jnp.bfloat16)
    grad_outw = contract(swished, d_branch, 0, 0)
    d_swished = contract(d_branch, w_out, 1, 1)
    d_pre = (d_swished * sig * (1.0 + pre_act * (1.0 - sig))).astype(jnp.bfloat16)
    grad_in = contract(hidden_activation, d_pre, 0, 0)
    hidden_gradient = contract(d_pre, w_in, 1, 1)
    gain1_gradient = lax.optimization_barrier(jnp.sum(hidden_gradient * normalized_input, axis=0))
    frames_gradient = residual_gradient + norm_input_gradient(hidden_gradient * layer_norm_gain1, normalized_input, inverse_deviation1)
    return (adapted, frames_gradient, grad_in, grad_outw, grad_adapt, gain1_gradient, grad_gain2)
```

```python
import functools

import jax
import jax.numpy as jnp
from jax import lax
from jax.experimental import pallas as pl
from jax.experimental.pallas import tpu as pltpu
from jax.sharding import PartitionSpec as P

EPS = 1e-05
BF = jnp.bfloat16
F32 = jnp.float32
MESH = pl.DeviceIdType.MESH
COPIES = 320


def wrap(value, size):
    return lax.rem(value + size, size)


class Place:
    def __init__(self):
        d, t = lax.axis_index("dp"), lax.axis_index("tensor")
        self.t = t
        self.at = {"x": d // 4, "z": d % 4, "y": t // 2, "c": t % 2}

    def shifted(self, axis, delta):
        return wrap(self.at[axis] + delta, 2 if axis == "c" else 4)

    def peer(self, axis, delta):
        if axis == "t":
            return {"tensor": wrap(self.t + delta, 8)}
        place = dict(self.at)
        place[axis] = self.shifted(axis, delta)
        if axis in ("x", "z"):
            return {"dp": place["x"] * 4 + place["z"]}
        return {"tensor": place["y"] * 2 + place["c"]}


class Net:
    def __init__(self, place, send, recv):
        self.place, self.send, self.recv = place, send, recv
        self.count = 0
        self.sent = []

    def copy(self, src, dst, axis, delta):
        number = self.count
        self.count += 1
        move = pltpu.make_async_remote_copy(
            src_ref=src,
            dst_ref=dst,
            send_sem=self.send.at[number],
            recv_sem=self.recv.at[number],
            device_id=self.place.peer(axis, delta),
            device_id_type=MESH,
        )
        move.start()
        self.sent.append(move)
        return number

    def arrived(self, number, ref):
        pltpu.make_async_remote_copy(
            src_ref=ref,
            dst_ref=ref,
            send_sem=self.send.at[number],
            recv_sem=self.recv.at[number],
            device_id=self.place.peer("c", 1),
            device_id_type=MESH,
        ).wait_recv()

    def drain(self):
        for move in self.sent:
            move.wait_send()


LOW, HIGH, ALL = pl.ds(0, 48), pl.ds(48, 48), slice(None)


class Gather:
    def __init__(self, net, src, buf, half, first, own, fine):
        self.net, self.src, self.buf, self.half, self.own, self.fine = net, src, buf, half, own, fine
        self.first, self.second = (first, "z" if first == "x" else "x")
        place = net.place
        self.p, self.q = place.at[self.first], place.at[self.second]

    def slot(self, i, j, rows=ALL):
        if self.first == "x":
            return self.buf.at[self.half, i, j, rows]
        return self.buf.at[self.half, j, i, rows]

    def ahead(self, delta):
        return self.net.place.shifted(self.first, delta)

    def across(self, delta):
        return self.net.place.shifted(self.second, delta)

    def both(self, src, dst, axis):
        return (self.net.copy(src, dst, axis, 1), self.net.copy(src, dst, axis, -1))

    def start(self):
        own = self.slot(self.p, self.q)
        self.one = self.both(self.src, own, self.first)
        self.waves = []
        if self.fine:
            self.waves.append((self.p, self.both(self.src, own, self.second)))

    def pass_on(self):
        net = self.net
        left, right = self.ahead(-1), self.ahead(1)
        net.arrived(self.one[0], self.slot(left, self.q))
        part = self.slot(left, self.q, LOW)
        low = net.copy(part, part, self.first, 1)
        net.arrived(self.one[1], self.slot(right, self.q))
        part = self.slot(right, self.q, HIGH)
        high = net.copy(part, part, self.first, -1)
        self.two = (low, high)
        if self.fine:
            for i in (left, right):
                self.wave(i)

    def wave(self, i):
        group = self.slot(i, self.q)
        self.waves.append((i, self.both(group, group, self.second)))

    def turn(self):
        far = self.ahead(2)
        self.net.arrived(self.two[0], self.slot(far, self.q, LOW))
        self.net.arrived(self.two[1], self.slot(far, self.q, HIGH))
        self.own.wait()
        self.wave(far if self.fine else ALL)

    def pass_across(self):
        net = self.net
        left, right = self.across(-1), self.across(1)
        self.last = []
        for i, numbers in self.waves:
            net.arrived(numbers[0], self.slot(i, left))
            part = self.slot(i, left, LOW)
            low = net.copy(part, part, self.second, 1)
            net.arrived(numbers[1], self.slot(i, right))
            part = self.slot(i, right, HIGH)
            high = net.copy(part, part, self.second, -1)
            self.last.append((i, low, high))

    def finish(self):
        far = self.across(2)
        for i, low, high in self.last:
            self.net.arrived(low, self.slot(i, far, LOW))
            self.net.arrived(high, self.slot(i, far, HIGH))


class Scatter:
    def __init__(self, net, buf, half, first, bufs, out, out_cols):
        self.net, self.buf, self.half = net, buf, half
        self.first, self.second = (first, "z" if first == "x" else "x")
        self.hop, self.near, self.total, self.hop2, self.near2 = bufs
        self.out, self.out_cols = out, out_cols

    def group(self, i, rows=ALL):
        if self.first == "x":
            return self.buf.at[self.half, i, :, rows]
        return self.buf.at[self.half, :, i, rows]

    def launch(self, block, hop, near, axis):
        net, place = self.net, self.net.place
        far, right, left = (place.shifted(axis, delta) for delta in (2, 1, -1))
        return (
            net.copy(block(far, LOW), hop(0), axis, 1),
            net.copy(block(far, HIGH), hop(1), axis, -1),
            net.copy(block(right, HIGH), near(0, HIGH), axis, 1),
            net.copy(block(left, LOW), near(1, LOW), axis, -1),
        )

    def relay(self, numbers, block, hop, near, axis):
        net, place = self.net, self.net.place
        right, left = place.shifted(axis, 1), place.shifted(axis, -1)
        net.arrived(numbers[0], hop(0))
        part = block(right, LOW)
        part[...] = (part[...].astype(F32) + hop(0)[...].astype(F32)).astype(BF)
        low = net.copy(part, near(0, LOW), axis, 1)
        net.arrived(numbers[1], hop(1))
        part = block(left, HIGH)
        part[...] = (part[...].astype(F32) + hop(1)[...].astype(F32)).astype(BF)
        high = net.copy(part, near(1, HIGH), axis, -1)
        return (low, high)

    def landed(self, numbers, more, near):
        net = self.net
        net.arrived(numbers[2], near(0, HIGH))
        net.arrived(more[0], near(0, LOW))
        net.arrived(numbers[3], near(1, LOW))
        net.arrived(more[1], near(1, HIGH))

    def hop_at(self, side):
        return self.hop.at[self.half, side]

    def near_at(self, side, rows=ALL):
        return self.near.at[self.half, side, :, rows]

    def total_at(self, j, rows=ALL):
        return self.total.at[self.half, j, rows]

    def hop2_at(self, side):
        return self.hop2.at[self.half, side]

    def near2_at(self, side, rows=ALL):
        return self.near2.at[self.half, side, rows]

    def start(self):
        self.one = self.launch(self.group, self.hop_at, self.near_at, self.first)

    def pass_on(self):
        self.two = self.relay(self.one, self.group, self.hop_at, self.near_at, self.first)

    def turn(self):
        self.landed(self.one, self.two, self.near_at)
        mine = self.group(self.net.place.at[self.first])
        total = mine[...].astype(F32) + self.near_at(0)[...].astype(F32) + self.near_at(1)[...].astype(F32)
        self.total[self.half] = total.astype(BF)
        self.three = self.launch(self.total_at, self.hop2_at, self.near2_at, self.second)

    def pass_across(self):
        self.four = self.relay(self.three, self.total_at, self.hop2_at, self.near2_at, self.second)

    def finish(self):
        self.landed(self.three, self.four, self.near2_at)
        mine = self.total_at(self.net.place.at[self.second])
        total = mine[...].astype(F32) + self.near2_at(0)[...].astype(F32) + self.near2_at(1)[...].astype(F32)
        self.out[:, self.out_cols] = total


class RowGather:
    def __init__(self, net, buf):
        self.net, self.buf = net, buf
        self.y, self.c = net.place.at["y"], net.place.at["c"]

    def start(self):
        net, own = self.net, self.buf.at[self.y, self.c]
        self.one = [(delta, net.copy(own, own, "y", delta)) for delta in (2, 1, -1)]
        self.side = [(self.y, net.copy(own, own, "c", 1))]

    def pass_on(self):
        net = self.net
        for delta, number in self.one[1:] + self.one[:1]:
            source = net.place.shifted("y", -delta)
            part = self.buf.at[source, self.c]
            net.arrived(number, part)
            self.side.append((source, net.copy(part, part, "c", 1)))

    def finish(self):
        other = 1 - self.c
        for source, number in self.side:
            self.net.arrived(number, self.buf.at[source, other])


class RowScatter:
    def __init__(self, net, part, side, sums, near):
        self.net, self.part, self.side, self.sums, self.near = net, part, side, sums, near
        self.y, self.c = net.place.at["y"], net.place.at["c"]

    def start(self):
        self.one = self.net.copy(self.part.at[:, 1 - self.c], self.side, "c", 1)

    def pair(self, row):
        return self.part[row, self.c].astype(F32) + self.side[row].astype(F32)

    def pass_on(self):
        net = self.net
        net.arrived(self.one, self.side)
        self.two = []
        for place, delta in enumerate((2, 1, -1)):
            self.sums[place] = self.pair(net.place.shifted("y", delta)).astype(BF)
            self.two.append(net.copy(self.sums.at[place], self.near.at[place], "y", delta))

    def finish(self):
        total = self.pair(self.y)
        for place, number in enumerate(self.two):
            self.net.arrived(number, self.near.at[place])
            total = total + self.near[place].astype(F32)
        return total


def row_norm(values):
    center = values - jnp.mean(values, axis=-1, keepdims=True)
    scale = lax.rsqrt(jnp.mean(center * center, axis=-1, keepdims=True) + EPS)
    return (center * scale, scale)


def row_norm_gradient(d_hat, vhat, scale):
    first = jnp.mean(d_hat, axis=-1, keepdims=True)
    second = jnp.mean(d_hat * vhat, axis=-1, keepdims=True)
    return scale * (d_hat - first - vhat * second)


def times(left, right):
    return jnp.dot(left, right, preferred_element_type=F32)


def times_t(left, right):
    return lax.dot_general(left, right, (((1,), (1,)), ((), ())), preferred_element_type=F32)


def kernel(
    frames, counts, gain1, gain2, w_in, w_out, w_ad, grad_out,
    adapted_o, fg_o, gin_o, gout_o, gad_o, gains_o,
    wi, wo, wa, gi, go, ga,
    hop_i, near_i, tot_i, hop2_i, near2_i,
    hop_o, near_o, tot_o, hop2_o, near2_o,
    hop_a, near_a, tot_a, hop2_a, near2_a,
    out_i, out_o, out_a,
    fr, rows, hid, nrm, dbr, across,
    part_b, side_b, sums_b, near_b,
    part_n, side_n, sums_n, near_n,
    part_h, side_h, sums_h, near_h,
    xhat, yhat, dres, cot, adapted, factor, swished, fgs, fgr,
    gn_c, gn_y, gn_x, gn_z, gn_out,
    send, recv, local,
):
    place = Place()
    net = Net(place, send, recv)
    x, z, y, c, t = place.at["x"], place.at["z"], place.at["y"], place.at["c"], place.t

    loads = []

    def load(src, dst):
        move = pltpu.make_async_copy(src, dst, local.at[len(loads)])
        move.start()
        loads.append(move)
        return move

    halves = {}
    for name, src, buf, width in (("i", w_in, wi, 256), ("o", w_out, wo, 256), ("a", w_ad, wa, 512)):
        for half in range(2):
            cut = src.at[:, pl.ds(half * width, width)]
            halves[name, half] = (cut, load(cut, buf.at[half, x, z]))
    cot_load = load(grad_out, cot)

    greeted = [("t", delta) for delta in range(1, 8)] + [(a, delta) for a in "xz" for delta in (1, -1, 2)]
    barrier = pltpu.get_barrier_semaphore()
    for axis, delta in greeted:
        pl.semaphore_signal(barrier, inc=1, device_id=place.peer(axis, delta), device_id_type=MESH)
    pl.semaphore_wait(barrier, len(greeted))

    frame_moves = [
        (delta, net.copy(frames.at[wrap(t + delta, 8)], fr.at[t], "t", delta)) for delta in range(1, 8)
    ]
    gathers = {}
    for name, buf in (("i", wi), ("o", wo), ("a", wa)):
        gathers[name] = []
        for half in range(2):
            src, own = halves[name, half]
            one = Gather(net, src, buf, half, "xz"[half], own, name == "i")
            one.start()
            gathers[name].append(one)

    def run(name, step):
        for one in gathers[name]:
            getattr(one, step)()

    fr[t] = frames[t]
    for delta, number in frame_moves:
        net.arrived(number, fr.at[wrap(t - delta, 8)])
    for piece in range(8):
        rows[:, piece * 192 : (piece + 1) * 192] = fr[piece].astype(F32)
    normal, rstd1 = row_norm(rows[...])
    xhat[...] = normal
    hid[y, c] = (normal * gain1[...]).astype(BF)
    hid_rows = RowGather(net, hid)
    hid_rows.start()

    run("i", "pass_on")
    run("o", "pass_on")
    run("i", "turn")
    run("o", "turn")

    cot_load.wait()
    live = lax.broadcasted_iota(jnp.int32, (256, 1), 0) < counts[0]
    cot[...] = jnp.where(live, cot[...].astype(F32), 0.0).astype(BF)

    run("i", "pass_across")
    hid_rows.pass_on()
    run("a", "pass_on")
    run("i", "finish")
    hid_rows.finish()

    def flat(ref):
        return ref[...].reshape(256, 1536)

    def front(half):
        pre = times(flat(hid), wi[half].reshape(1536, 256))
        sig = jax.nn.sigmoid(pre)
        swished[half] = (pre * sig).astype(BF)
        factor[half] = sig * (1.0 + pre * (1.0 - sig))

    front(0)
    front(1)
    run("a", "turn")
    run("o", "pass_across")
    run("o", "finish")

    def rows_out(part, left, weight):
        def body(i, carry):
            value = times_t(left(0), weight[0, i].reshape(384, -1))
            value = value + times_t(left(1), weight[1, i].reshape(384, -1))
            columns = pl.ds(pl.multiple_of(i * 384, 128), 384)
            part[:, :, :, columns] = value.astype(BF).reshape(4, 2, 32, 384)
            return carry

        lax.fori_loop(0, 4, body, 0)

    rows_out(part_b, lambda half: swished[half], wo)
    branch = RowScatter(net, part_b, side_b, sums_b, near_b)
    branch.start()
    branch.pass_on()
    run("a", "pass_across")

    resid = rows[...] + 0.5 * branch.finish()
    normal, rstd2 = row_norm(resid)
    yhat[...] = normal
    nrm[y, c] = (normal * gain2[...]).astype(BF)
    nrm_rows = RowGather(net, nrm)
    nrm_rows.start()

    run("a", "finish")
    rows_out(part_n, lambda half: cot[:, half * 512 : (half + 1) * 512], wa)
    d_norm = RowScatter(net, part_n, side_n, sums_n, near_n)
    d_norm.start()
    nrm_rows.pass_on()
    d_norm.pass_on()
    nrm_rows.finish()

    def outer(grad, half, right):
        def body(i, carry):
            left = across[pl.ds(pl.multiple_of(i * 384, 128), 384), :]
            grad[half, i] = times(left, right).astype(BF).reshape(4, 96, -1)
            return carry

        lax.fori_loop(0, 4, body, 0)

    def scatter(buf, bufs, out, width):
        return [
            Scatter(net, buf, half, "zx"[half], bufs, out, pl.ds(half * width, width)) for half in range(2)
        ]

    sc_a = scatter(ga, (hop_a, near_a, tot_a, hop2_a, near2_a), out_a, 512)
    sc_o = scatter(go, (hop_o, near_o, tot_o, hop2_o, near2_o), out_o, 256)
    sc_i = scatter(gi, (hop_i, near_i, tot_i, hop2_i, near2_i), out_i, 256)

    def step(ones, name):
        for one in ones:
            getattr(one, name)()

    across[...] = flat(nrm).T
    for half in range(2):
        outer(ga, half, cot[:, half * 512 : (half + 1) * 512])
        sc_a[half].start()

    for half in range(2):
        value = times(flat(nrm), wa[half].reshape(1536, 512))
        adapted[:, half * 512 : (half + 1) * 512] = jnp.where(live, value, 0.0).astype(BF)
    stores = [load(adapted, adapted_o)]

    d_normed = d_norm.finish()
    gain2_part = jnp.sum(d_normed * yhat[...], axis=0, keepdims=True)
    d_resid = row_norm_gradient(d_normed * gain2[...], yhat[...], rstd2)
    dres[...] = d_resid
    dbr[y, c] = (0.5 * d_resid).astype(BF)
    dbr_rows = RowGather(net, dbr)
    dbr_rows.start()
    step(sc_a, "pass_on")
    dbr_rows.pass_on()
    dbr_rows.finish()

    pres = []
    for half in range(2):
        d_swished = times(flat(dbr), wo[half].reshape(1536, 256))
        pres.append((d_swished * factor[half]).astype(BF))
    rows_out(part_h, lambda half: pres[half], wi)
    d_hid = RowScatter(net, part_h, side_h, sums_h, near_h)
    d_hid.start()
    across[...] = flat(dbr).T
    for half in range(2):
        outer(go, half, swished[half])
        sc_o[half].start()
    d_hid.pass_on()
    across[...] = flat(hid).T
    for half in range(2):
        outer(gi, half, pres[half])
        sc_i[half].start()
    step(sc_a, "turn")

    d_hidden = d_hid.finish()
    gn_c[c] = jnp.concatenate([jnp.sum(d_hidden * xhat[...], axis=0, keepdims=True), gain2_part], axis=0)
    gain_move = net.copy(gn_c.at[c], gn_c.at[c], "c", 1)
    grad_rows = dres[...] + row_norm_gradient(d_hidden * gain1[...], xhat[...], rstd1)
    for piece in range(8):
        fgs[piece] = grad_rows[:, piece * 192 : (piece + 1) * 192]
    fgr[t] = fgs[t]
    grad_moves = [
        (delta, net.copy(fgs.at[wrap(t + delta, 8)], fgr.at[t], "t", delta)) for delta in range(1, 8)
    ]

    net.arrived(gain_move, gn_c.at[1 - c])
    total = gn_c[0] + gn_c[1]

    def gain_start(buf, axis, total):
        own = place.at[axis]
        buf[own] = total
        return [(delta, net.copy(buf.at[own], buf.at[own], axis, delta)) for delta in (1, -1, 2)]

    def gain_sum(moves, buf, axis):
        for delta, number in moves:
            net.arrived(number, buf.at[place.shifted(axis, -delta)])
        return buf[0] + buf[1] + buf[2] + buf[3]

    moves = gain_start(gn_y, "y", total)
    step(sc_a, "pass_across")
    step(sc_o, "pass_on")
    total = gain_sum(moves, gn_y, "y")
    moves = gain_start(gn_x, "x", total)
    step(sc_i, "pass_on")
    total = gain_sum(moves, gn_x, "x")
    moves = gain_start(gn_z, "z", total)
    step(sc_a, "finish")
    stores.append(load(out_a, gad_o))
    step(sc_o, "turn")
    step(sc_i, "turn")
    for delta, number in grad_moves:
        net.arrived(number, fgr.at[wrap(t - delta, 8)])
    stores.append(load(fgr, fg_o))
    gn_out[...] = gain_sum(moves, gn_z, "z")
    stores.append(load(gn_out, gains_o))
    step(sc_o, "pass_across")
    step(sc_i, "pass_across")
    step(sc_o, "finish")
    stores.append(load(out_o, gout_o))
    step(sc_i, "finish")
    stores.append(load(out_i, gin_o))
    net.drain()
    for move in stores:
        move.wait()


def on_device(frames, counts, layer_norm_gain1, w_in, w_out, norm_gain2, w_adapt, grad_out):
    def weight(width):
        return pltpu.VMEM((2, 4, 4, 96, width), BF)

    def sums(width):
        return [
            pltpu.VMEM((2, 2, 4, 48, width), BF),
            pltpu.VMEM((2, 2, 4, 96, width), BF),
            pltpu.VMEM((2, 4, 96, width), BF),
            pltpu.VMEM((2, 2, 48, width), BF),
            pltpu.VMEM((2, 2, 96, width), BF),
        ]

    slots = pltpu.VMEM((4, 2, 32, 1536), BF)
    row_sums = [
        slots,
        pltpu.VMEM((4, 32, 1536), BF),
        pltpu.VMEM((3, 32, 1536), BF),
        pltpu.VMEM((3, 32, 1536), BF),
    ]
    scratch = (
        [weight(256), weight(256), weight(512)] * 2
        + sums(256)
        + sums(256)
        + sums(512)
        + [pltpu.VMEM((96, 512), F32), pltpu.VMEM((96, 512), F32), pltpu.VMEM((96, 1024), F32)]
        + [pltpu.VMEM((8, 32, 192), BF), pltpu.VMEM((32, 1536), F32)]
        + [slots] * 3
        + [pltpu.VMEM((1536, 256), BF)]
        + row_sums * 3
        + [pltpu.VMEM((32, 1536), F32)] * 3
        + [pltpu.VMEM((256, 1024), BF), pltpu.VMEM((256, 1024), BF)]
        + [pltpu.VMEM((2, 256, 256), F32), pltpu.VMEM((2, 256, 256), BF)]
        + [pltpu.VMEM((8, 32, 192), F32)] * 2
        + [pltpu.VMEM((2, 2, 1536), F32)]
        + [pltpu.VMEM((4, 2, 1536), F32)] * 3
        + [pltpu.VMEM((2, 1536), F32)]
        + [pltpu.SemaphoreType.DMA((COPIES,)), pltpu.SemaphoreType.DMA((COPIES,)), pltpu.SemaphoreType.DMA((16,))]
    )
    vmem, far = pl.BlockSpec(memory_space=pltpu.VMEM), pl.BlockSpec(memory_space=pl.ANY)
    shape = jax.ShapeDtypeStruct
    adapted, fg, gin, gout, gad, gains = pl.pallas_call(
        kernel,
        out_shape=(
            shape((256, 1024), BF),
            shape((8, 32, 192), F32),
            shape((96, 512), F32),
            shape((96, 512), F32),
            shape((96, 1024), F32),
            shape((2, 1536), F32),
        ),
        in_specs=[vmem, pl.BlockSpec(memory_space=pltpu.SMEM), vmem, vmem, far, far, far, far],
        out_specs=[far] * 6,
        scratch_shapes=scratch,
        compiler_params=pltpu.CompilerParams(
            collective_id=0, has_side_effects=True, vmem_limit_bytes=58 * 2**20
        ),
    )(
        frames.reshape(8, 32, 192),
        counts,
        layer_norm_gain1.reshape(1, 1536),
        norm_gain2.reshape(1, 1536),
        w_in,
        w_out.T,
        w_adapt,
        grad_out,
    )
    return (adapted, fg.reshape(256, 192), gin, gout.T, gad, gains[0], gains[1])


def solution(mesh):
    return jax.shard_map(
        on_device,
        mesh=mesh,
        in_specs=(
            P("dp", "tensor"),
            P("dp"),
            P(),
            P("dp", "tensor"),
            P("tensor", "dp"),
            P(),
            P("dp", "tensor"),
            P("dp", "tensor"),
        ),
        out_specs=(
            P("dp", "tensor"),
            P("dp", "tensor"),
            P("dp", "tensor"),
            P("tensor", "dp"),
            P("dp", "tensor"),
            P(),
            P(),
        ),
        check_vma=False,
    )
```

```python
import functools

import jax
import jax.numpy as jnp
from jax import lax
from jax.experimental import pallas as pl
from jax.experimental.pallas import tpu as pltpu
from jax.sharding import PartitionSpec as P

EPS = 1e-05
BF = jnp.bfloat16
F32 = jnp.float32
MESH = pl.DeviceIdType.MESH
LANES = 116


def wrap(value, size):
    return lax.rem(value + size, size)


class Place:
    def __init__(self):
        d, t = lax.axis_index("dp"), lax.axis_index("tensor")
        self.t = t
        self.at = {"x": d // 4, "z": d % 4, "y": t // 2, "c": t % 2}

    def shifted(self, axis, delta):
        return wrap(self.at[axis] + delta, 2 if axis == "c" else 4)

    def peer(self, axis, delta):
        if axis == "t":
            return {"tensor": wrap(self.t + delta, 8)}
        place = dict(self.at)
        place[axis] = self.shifted(axis, delta)
        if axis in ("x", "z"):
            return {"dp": place["x"] * 4 + place["z"]}
        return {"tensor": place["y"] * 2 + place["c"]}


class Net:
    def __init__(self, place, sems):
        self.place, self.sems = place, sems
        self.lanes = 0
        self.sent = []

    def lane(self):
        self.lanes += 1
        return self.lanes - 1

    def out_lane(self, gauge):
        lane = self.lane()
        self.sent.append((lane, gauge))
        return lane

    def copy(self, src, dst, axis, delta, out, into):
        pltpu.make_async_remote_copy(
            src_ref=src,
            dst_ref=dst,
            send_sem=self.sems.at[out],
            recv_sem=self.sems.at[into],
            device_id=self.place.peer(axis, delta),
            device_id_type=MESH,
        ).start()

    def whole(self, lane, gauge):
        return pltpu.make_async_remote_copy(
            src_ref=gauge,
            dst_ref=gauge,
            send_sem=self.sems.at[lane],
            recv_sem=self.sems.at[lane],
            device_id=self.place.peer("c", 1),
            device_id_type=MESH,
        )

    def arrived(self, lane, gauge):
        self.whole(lane, gauge).wait_recv()

    def drain(self):
        for lane, gauge in self.sent:
            self.whole(lane, gauge).wait_send()


LOW, HIGH, ALL = pl.ds(0, 48), pl.ds(48, 48), slice(None)


class Gather:
    def __init__(self, net, src, buf, half, first, own):
        self.net, self.src, self.buf, self.half, self.own = net, src, buf, half, own
        self.first, self.second = (first, "z" if first == "x" else "x")
        place = net.place
        self.p, self.q = place.at[self.first], place.at[self.second]
        self.out = net.out_lane(buf.at[half, pl.ds(0, 15)])
        self.near, self.far, self.last = net.lane(), net.lane(), net.lane()
        self.waves = [net.lane() for _ in range(3)]

    def slot(self, i, j, rows=ALL):
        return self.buf.at[self.half, i * 4 + j if self.first == "x" else j * 4 + i, rows]

    def wait(self, lane, blocks):
        self.net.arrived(lane, self.buf.at[self.half, pl.ds(0, blocks)])

    def both(self, src, dst, axis, lane):
        for delta in (1, -1):
            self.net.copy(src, dst, axis, delta, self.out, lane)

    def relay(self, slot, axis, lane):
        left, right = self.net.place.shifted(axis, -1), self.net.place.shifted(axis, 1)
        self.net.copy(slot(left, LOW), slot(left, LOW), axis, 1, self.out, lane)
        self.net.copy(slot(right, HIGH), slot(right, HIGH), axis, -1, self.out, lane)

    def ahead(self, delta):
        return self.net.place.shifted(self.first, delta)

    def wave(self, i, lane):
        block = self.slot(i, self.q)
        self.both(block, block, self.second, lane)

    def start(self):
        own = self.slot(self.p, self.q)
        self.both(self.src, own, self.first, self.near)
        self.both(self.src, own, self.second, self.waves[0])

    def pass_on(self):
        self.wait(self.near, 2)
        self.relay(lambda i, rows: self.slot(i, self.q, rows), self.first, self.far)
        self.wave(self.ahead(-1), self.waves[1])
        self.wave(self.ahead(1), self.waves[1])

    def turn(self):
        self.wait(self.far, 1)
        self.wave(self.ahead(2), self.waves[2])

    def across(self, i):
        self.relay(lambda j, rows: self.slot(i, j, rows), self.second, self.last)

    def across_own(self):
        self.wait(self.waves[0], 2)
        self.across(self.p)

    def across_next(self):
        self.wait(self.waves[1], 4)
        self.across(self.ahead(-1))
        self.across(self.ahead(1))

    def across_far(self):
        self.wait(self.waves[2], 2)
        self.across(self.ahead(2))

    def finish(self):
        self.wait(self.last, 4)
        self.own.wait()


class Scatter:
    def __init__(self, net, buf, half, first, bufs, gauge, out, out_cols):
        self.net, self.buf, self.half = net, buf, half
        self.first, self.second = (first, "z" if first == "x" else "x")
        self.hop, self.near, self.total, self.hop2, self.near2 = bufs
        self.out, self.out_cols = out, out_cols
        self.sends = net.out_lane(gauge.at[half, pl.ds(0, 15)])
        self.lanes = [net.lane() for _ in range(4)]

    def group(self, i, rows=ALL):
        if self.first == "x":
            return self.buf.at[self.half, i, :, rows]
        return self.buf.at[self.half, :, i, rows]

    def launch(self, block, hop, near, axis, lanes):
        place = self.net.place
        far, right, left = (place.shifted(axis, delta) for delta in (2, 1, -1))
        self.net.copy(block(far, LOW), hop(0), axis, 1, self.sends, lanes[0])
        self.net.copy(block(far, HIGH), hop(1), axis, -1, self.sends, lanes[0])
        self.net.copy(block(right, HIGH), near(0, HIGH), axis, 1, self.sends, lanes[1])
        self.net.copy(block(left, LOW), near(1, LOW), axis, -1, self.sends, lanes[1])

    def relay(self, block, hop, near, axis, lanes):
        place = self.net.place
        right, left = place.shifted(axis, 1), place.shifted(axis, -1)
        for side, part, rows, delta in ((0, block(right, LOW), LOW, 1), (1, block(left, HIGH), HIGH, -1)):
            part[...] = (part[...].astype(F32) + hop(side)[...].astype(F32)).astype(BF)
            self.net.copy(part, near(side, rows), axis, delta, self.sends, lanes[1])

    def hop_at(self, side):
        return self.hop.at[self.half, side]

    def near_at(self, side, rows=ALL):
        return self.near.at[self.half, side, :, rows]

    def total_at(self, j, rows=ALL):
        return self.total.at[self.half, j, rows]

    def hop2_at(self, side):
        return self.hop2.at[self.half, side]

    def near2_at(self, side, rows=ALL):
        return self.near2.at[self.half, side, rows]

    def start(self):
        self.launch(self.group, self.hop_at, self.near_at, self.first, self.lanes[:2])

    def pass_on(self):
        self.net.arrived(self.lanes[0], self.hop.at[self.half])
        self.relay(self.group, self.hop_at, self.near_at, self.first, self.lanes[:2])

    def turn(self):
        self.net.arrived(self.lanes[1], self.near.at[self.half])
        mine = self.group(self.net.place.at[self.first])
        total = mine[...].astype(F32) + self.near_at(0)[...].astype(F32) + self.near_at(1)[...].astype(F32)
        self.total[self.half] = total.astype(BF)
        self.launch(self.total_at, self.hop2_at, self.near2_at, self.second, self.lanes[2:])

    def pass_across(self):
        self.net.arrived(self.lanes[2], self.hop2.at[self.half])
        self.relay(self.total_at, self.hop2_at, self.near2_at, self.second, self.lanes[2:])

    def finish(self):
        self.net.arrived(self.lanes[3], self.near2.at[self.half])
        mine = self.total_at(self.net.place.at[self.second])
        total = mine[...].astype(F32) + self.near2_at(0)[...].astype(F32) + self.near2_at(1)[...].astype(F32)
        self.out[:, self.out_cols] = total


class RowGather:
    def __init__(self, net, buf):
        self.net, self.buf = net, buf
        self.y, self.c = net.place.at["y"], net.place.at["c"]
        self.out = net.out_lane(buf.at[pl.ds(0, 7)])
        self.near, self.far, self.side = net.lane(), net.lane(), net.lane()

    def slot(self, delta):
        return self.buf.at[self.net.place.shifted("y", delta) * 2 + self.c]

    def beside(self, delta):
        self.net.copy(self.slot(delta), self.slot(delta), "c", 1, self.out, self.side)

    def start(self):
        for delta in (1, -1, 2):
            lane = self.far if delta == 2 else self.near
            self.net.copy(self.slot(0), self.slot(0), "y", delta, self.out, lane)
        self.beside(0)

    def pass_near(self):
        self.net.arrived(self.near, self.buf.at[pl.ds(0, 2)])
        self.beside(-1)
        self.beside(1)

    def pass_far(self):
        self.net.arrived(self.far, self.slot(2))
        self.beside(2)

    def finish(self):
        self.net.arrived(self.side, self.buf.at[pl.ds(0, 4)])


class RowScatter:
    def __init__(self, net, bufs):
        self.net = net
        self.part, self.side, self.sums, self.near = bufs
        self.y, self.c = net.place.at["y"], net.place.at["c"]
        self.beside, self.out = net.out_lane(self.side), net.out_lane(self.sums)
        self.one = [net.lane() for _ in range(2)]
        self.two = [net.lane() for _ in range(2)]

    def put(self, i, value):
        self.part[i] = value.reshape(4, 2, 32, 384)
        self.net.copy(self.part.at[i, :, 1 - self.c], self.side.at[i], "c", 1, self.beside, self.one[i // 2])

    def pair(self, i, row):
        return self.part[i, row, self.c] + self.side[i, row]

    def pass_on(self, piece):
        net = self.net
        net.arrived(self.one[piece], self.side.at[pl.ds(2 * piece, 2)])
        for place, delta in enumerate((1, -1, 2)):
            row = net.place.shifted("y", delta)
            for k in range(2):
                self.sums[piece, place, :, k * 384 : (k + 1) * 384] = self.pair(2 * piece + k, row).astype(BF)
            net.copy(
                self.sums.at[piece, place], self.near.at[piece, place], "y", delta, self.out, self.two[piece]
            )

    def finish(self):
        halves = []
        for piece in range(2):
            total = jnp.concatenate([self.pair(2 * piece, self.y), self.pair(2 * piece + 1, self.y)], axis=1)
            self.net.arrived(self.two[piece], self.near.at[piece])
            for place in range(3):
                total = total + self.near[piece, place].astype(F32)
            halves.append(total)
        return jnp.concatenate(halves, axis=1)


def row_norm(values):
    center = values - jnp.mean(values, axis=-1, keepdims=True)
    scale = lax.rsqrt(jnp.mean(center * center, axis=-1, keepdims=True) + EPS)
    return (center * scale, scale)


def row_norm_gradient(d_hat, vhat, scale):
    first = jnp.mean(d_hat, axis=-1, keepdims=True)
    second = jnp.mean(d_hat * vhat, axis=-1, keepdims=True)
    return scale * (d_hat - first - vhat * second)


def times(left, right):
    return jnp.dot(left, right, preferred_element_type=F32)


def times_t(left, right):
    return lax.dot_general(left, right, (((1,), (1,)), ((), ())), preferred_element_type=F32)


def kernel(
    frames_in, counts, gain1_in, gain2_in, w_in, w_out, w_ad, grad_out,
    adapted_o, fg_o, gin_o, gout_o, gad_o, gain1_o, gain2_o,
    wi, wo, wa, gi, go, ga,
    hop_i, near_i, tot_i, hop2_i, near2_i,
    hop_o, near_o, tot_o, hop2_o, near2_o,
    hop_a, near_a, tot_a, hop2_a, near2_a,
    out_i, out_o, out_a,
    frames, gain1_v, gain2_v, own, fg,
    fr, rows, hid, nrm, dbr, hid_t, nrm_t, dbr_t,
    part_b, side_b, sums_b, near_b,
    part_n, side_n, sums_n, near_n,
    part_h, side_h, sums_h, near_h,
    xhat, yhat, dres, cot, adapted, factor, swished, fgs, fgr,
    gn_c, gn_y, gn_x, gn_z, gn_1, gn_2,
    sems, local,
):
    place = Place()
    net = Net(place, sems)
    x, z, y, c, t = place.at["x"], place.at["z"], place.at["y"], place.at["c"], place.t

    greeted = [("t", delta) for delta in range(1, 8)] + [(a, delta) for a in "xz" for delta in (1, -1, 2)]
    barrier = pltpu.get_barrier_semaphore()
    for axis, delta in greeted:
        pl.semaphore_signal(barrier, inc=1, device_id=place.peer(axis, delta), device_id_type=MESH)

    loads = []

    def load(src, dst):
        move = pltpu.make_async_copy(src, dst, local.at[len(loads)])
        move.start()
        loads.append(move)
        return move

    frames_load = load(frames_in, frames)
    gain_loads = [load(gain1_in, gain1_v), load(gain2_in, gain2_v)]
    gathers = []
    for src, buf, width in ((w_in, wi, 256), (w_out, wo, 256), (w_ad, wa, 512)):
        for half in range(2):
            cut = src.at[:, pl.ds(half * width, width)]
            gathers.append(Gather(net, cut, buf, half, "xz"[half], load(cut, buf.at[half, x * 4 + z])))
    i0, i1, o0, o1, a0, a1 = gathers
    cot_load = load(grad_out, cot)
    frames_load.wait()
    own[...] = frames[...].T.reshape(8, 32, 192)
    pl.semaphore_wait(barrier, len(greeted))

    def to_peers(src, dst, out, into):
        for delta in range(1, 8):
            net.copy(src.at[wrap(t + delta, 8)], dst.at[t], "t", delta, out, into)

    frames_lane = net.lane()
    to_peers(own, fr, net.out_lane(own.at[pl.ds(0, 7)]), frames_lane)
    i0.start()
    i1.start()
    cot_load.wait()
    live = lax.broadcasted_iota(jnp.int32, (256, 1), 0) < counts[0]
    cot[...] = jnp.where(live, cot[...].astype(F32), 0.0).astype(BF)

    fr[t] = own[t]
    for one in gain_loads:
        one.wait()
    gain1, gain2 = gain1_v[...].reshape(1, 1536), gain2_v[...].reshape(1, 1536)
    net.arrived(frames_lane, fr.at[pl.ds(0, 7)])
    for piece in range(8):
        rows[:, piece * 192 : (piece + 1) * 192] = fr[piece].astype(F32)
    normal, rstd1 = row_norm(rows[...])
    xhat[...] = normal
    hid[t] = (normal * gain1).astype(BF)
    hid_rows = RowGather(net, hid)
    hid_rows.start()

    i0.pass_on()
    i0.across_own()
    o0.start()
    o1.start()
    i1.pass_on()
    i1.across_own()
    i0.turn()
    o0.pass_on()
    i0.across_next()
    o1.across_own()
    o0.across_own()
    hid_rows.pass_near()
    hid_rows.pass_far()
    i1.across_next()
    o1.pass_on()
    hid_rows.finish()
    i1.turn()

    def flat(ref):
        return ref[...].reshape(256, 1536)

    hid_t[...] = flat(hid).T
    o0.turn()
    i0.across_far()
    o0.across_next()
    o1.across_next()
    o1.turn()
    a0.start()
    i1.across_far()
    a1.start()
    o0.across_far()

    def front(half):
        pre = times(flat(hid), wi[half].reshape(1536, 256))
        sig = jax.nn.sigmoid(pre)
        swished[half] = (pre * sig).astype(BF)
        factor[half] = sig * (1.0 + pre * (1.0 - sig))

    i0.finish()
    front(0)
    o1.across_far()
    a0.across_own()
    a0.pass_on()
    i1.finish()
    front(1)
    a1.pass_on()
    o0.finish()
    a1.across_own()
    o1.finish()

    def rows_out(scatter, left, weight):
        for i in range(4):
            some = slice(4 * i, 4 * i + 4)
            value = times_t(left(0), weight[0, some].reshape(384, -1))
            value = value + times_t(left(1), weight[1, some].reshape(384, -1))
            scatter.put(i, value)

    branch = RowScatter(net, (part_b, side_b, sums_b, near_b))
    rows_out(branch, lambda half: swished[half], wo)
    a0.turn()
    branch.pass_on(0)
    branch.pass_on(1)
    a0.across_next()
    a1.turn()
    a1.across_next()
    a0.across_far()

    resid = rows[...] + 0.5 * branch.finish()
    normal, rstd2 = row_norm(resid)
    yhat[...] = normal
    nrm[t] = (normal * gain2).astype(BF)
    nrm_rows = RowGather(net, nrm)
    nrm_rows.start()

    a1.across_far()
    a0.finish()
    a1.finish()
    d_norm = RowScatter(net, (part_n, side_n, sums_n, near_n))
    rows_out(d_norm, lambda half: cot[:, half * 512 : (half + 1) * 512], wa)
    d_norm.pass_on(0)
    nrm_rows.pass_near()
    nrm_rows.pass_far()
    d_norm.pass_on(1)
    nrm_rows.finish()

    def outer(grad, half, left, right):
        def body(i, carry):
            some = left[pl.ds(pl.multiple_of(i * 384, 128), 384), :]
            grad[half, i] = times(some, right).astype(BF).reshape(4, 96, -1)
            return carry

        lax.fori_loop(0, 4, body, 0)

    def scatter(buf, bufs, gauge, out, width):
        return [
            Scatter(net, buf, half, "zx"[half], bufs, gauge, out, pl.ds(half * width, width))
            for half in range(2)
        ]

    sa0, sa1 = scatter(ga, (hop_a, near_a, tot_a, hop2_a, near2_a), wa, out_a, 512)
    so0, so1 = scatter(go, (hop_o, near_o, tot_o, hop2_o, near2_o), wo, out_o, 256)
    si0, si1 = scatter(gi, (hop_i, near_i, tot_i, hop2_i, near2_i), wi, out_i, 256)

    nrm_t[...] = flat(nrm).T
    outer(ga, 0, nrm_t, cot[:, :512])
    sa0.start()
    outer(ga, 1, nrm_t, cot[:, 512:])
    sa1.start()

    for half in range(2):
        value = times(flat(nrm), wa[half].reshape(1536, 512))
        adapted[:, half * 512 : (half + 1) * 512] = jnp.where(live, value, 0.0).astype(BF)
    stores = [load(adapted, adapted_o)]

    d_normed = d_norm.finish()
    gain2_part = jnp.sum(d_normed * yhat[...], axis=0, keepdims=True)
    d_resid = row_norm_gradient(d_normed * gain2, yhat[...], rstd2)
    dres[...] = d_resid
    dbr[t] = (0.5 * d_resid).astype(BF)
    dbr_rows = RowGather(net, dbr)
    dbr_rows.start()
    sa0.pass_on()
    sa1.pass_on()
    dbr_rows.pass_near()
    dbr_rows.pass_far()
    dbr_rows.finish()

    dbr_t[...] = flat(dbr).T
    outer(go, 0, dbr_t, swished[0])
    so0.start()
    outer(go, 1, dbr_t, swished[1])
    so1.start()
    pres = []
    for half in range(2):
        d_swished = times(flat(dbr), wo[half].reshape(1536, 256))
        pres.append((d_swished * factor[half]).astype(BF))
    outer(gi, 0, hid_t, pres[0])
    si0.start()
    outer(gi, 1, hid_t, pres[1])
    si1.start()
    d_hid = RowScatter(net, (part_h, side_h, sums_h, near_h))
    rows_out(d_hid, lambda half: pres[half], wi)
    sa0.turn()
    d_hid.pass_on(0)
    d_hid.pass_on(1)
    sa1.turn()
    so0.pass_on()
    so1.pass_on()
    si0.pass_on()
    si1.pass_on()
    sa1.pass_across()

    d_hidden = d_hid.finish()
    gn_c[c] = jnp.concatenate([jnp.sum(d_hidden * xhat[...], axis=0, keepdims=True), gain2_part], axis=0)
    lane = net.lane()
    net.copy(gn_c.at[c], gn_c.at[c], "c", 1, net.out_lane(gn_c.at[0]), lane)
    grad_rows = dres[...] + row_norm_gradient(d_hidden * gain1, xhat[...], rstd1)
    for piece in range(8):
        fgs[piece] = grad_rows[:, piece * 192 : (piece + 1) * 192]
    fgr[t] = fgs[t]
    rows_lane = net.lane()
    to_peers(fgs, fgr, net.out_lane(fgs.at[pl.ds(0, 7)]), rows_lane)
    net.arrived(lane, gn_c.at[1 - c])
    total = gn_c[0] + gn_c[1]

    def gain_start(buf, axis, total):
        here = buf.at[place.at[axis]]
        here[...] = total
        out, into = net.out_lane(buf.at[pl.ds(0, 3)]), net.lane()
        for delta in (1, -1, 2):
            net.copy(here, here, axis, delta, out, into)
        return into

    def gain_sum(into, buf):
        net.arrived(into, buf.at[pl.ds(0, 3)])
        return buf[0] + buf[1] + buf[2] + buf[3]

    lane = gain_start(gn_y, "y", total)
    sa0.pass_across()
    so0.turn()
    so1.turn()
    lane = gain_start(gn_x, "x", gain_sum(lane, gn_y))
    net.arrived(rows_lane, fgr.at[pl.ds(0, 7)])
    fg[...] = fgr[...].reshape(256, 192).T
    stores.append(load(fg, fg_o))
    si0.turn()
    si1.turn()
    lane = gain_start(gn_z, "z", gain_sum(lane, gn_x))
    sa0.finish()
    sa1.finish()
    stores.append(load(out_a, gad_o))
    so0.pass_across()
    so1.pass_across()
    si0.pass_across()
    si1.pass_across()
    so0.finish()
    so1.finish()
    stores.append(load(out_o, gout_o))
    total = gain_sum(lane, gn_z)
    gn_1[...] = total[0]
    gn_2[...] = total[1]
    stores.append(load(gn_1, gain1_o))
    stores.append(load(gn_2, gain2_o))
    si0.finish()
    si1.finish()
    stores.append(load(out_i, gin_o))
    net.drain()
    for move in stores:
        move.wait()


def hand_over(*refs):
    count = len(refs) // 3
    sems = refs[-1]
    moves = []
    for i in range(count):
        hold = refs[2 * count + i]
        moves.append(
            (
                pltpu.make_async_copy(refs[i], hold, sems.at[0, i]),
                pltpu.make_async_copy(hold, refs[count + i], sems.at[1, i]),
            )
        )
        moves[-1][0].start()
    for come, go in moves:
        come.wait()
        go.start()
    for come, go in moves:
        go.wait()


def on_device(frames, counts, layer_norm_gain1, w_in, w_out, norm_gain2, w_adapt, grad_out):
    def weight(width):
        return pltpu.VMEM((2, 16, 96, width), BF)

    def gradient(width):
        return pltpu.VMEM((2, 4, 4, 96, width), BF)

    def sums(width):
        return [
            pltpu.VMEM((2, 2, 4, 48, width), BF),
            pltpu.VMEM((2, 2, 4, 96, width), BF),
            pltpu.VMEM((2, 4, 96, width), BF),
            pltpu.VMEM((2, 2, 48, width), BF),
            pltpu.VMEM((2, 2, 96, width), BF),
        ]

    slots = pltpu.VMEM((8, 32, 1536), BF)
    row_sums = [
        pltpu.VMEM((4, 4, 2, 32, 384), F32),
        pltpu.VMEM((4, 4, 32, 384), F32),
        pltpu.VMEM((2, 3, 32, 768), BF),
        pltpu.VMEM((2, 3, 32, 768), BF),
    ]
    scratch = (
        [weight(256), weight(256), weight(512), gradient(256), gradient(256), gradient(512)]
        + sums(256)
        + sums(256)
        + sums(512)
        + [pltpu.VMEM((96, 512), F32), pltpu.VMEM((96, 512), F32), pltpu.VMEM((96, 1024), F32)]
        + [pltpu.VMEM((192, 256), BF), pltpu.VMEM((1536,), F32), pltpu.VMEM((1536,), F32)]
        + [pltpu.VMEM((8, 32, 192), BF), pltpu.VMEM((192, 256), F32)]
        + [pltpu.VMEM((8, 32, 192), BF), pltpu.VMEM((32, 1536), F32)]
        + [slots] * 3
        + [pltpu.VMEM((1536, 256), BF)] * 3
        + row_sums * 3
        + [pltpu.VMEM((32, 1536), F32)] * 3
        + [pltpu.VMEM((256, 1024), BF), pltpu.VMEM((256, 1024), BF)]
        + [pltpu.VMEM((2, 256, 256), F32), pltpu.VMEM((2, 256, 256), BF)]
        + [pltpu.VMEM((8, 32, 192), F32)] * 2
        + [pltpu.VMEM((2, 2, 1536), F32)]
        + [pltpu.VMEM((4, 2, 1536), F32)] * 3
        + [pltpu.VMEM((1536,), F32)] * 2
        + [pltpu.SemaphoreType.DMA((LANES,)), pltpu.SemaphoreType.DMA((17,))]
    )
    far = pl.BlockSpec(memory_space=pl.ANY)
    shape = jax.ShapeDtypeStruct
    shapes = (
        shape((256, 1024), BF),
        shape((192, 256), F32),
        shape((96, 512), F32),
        shape((96, 512), F32),
        shape((96, 1024), F32),
        shape((1536,), F32),
        shape((1536,), F32),
    )
    results = pl.pallas_call(
        kernel,
        out_shape=shapes,
        in_specs=[far, pl.BlockSpec(memory_space=pltpu.SMEM)] + [far] * 6,
        out_specs=[far] * 7,
        scratch_shapes=scratch,
        compiler_params=pltpu.CompilerParams(
            collective_id=0, has_side_effects=True, vmem_limit_bytes=58 * 2**20
        ),
    )(
        frames.T,
        counts,
        layer_norm_gain1,
        norm_gain2,
        w_in,
        w_out.T,
        w_adapt,
        grad_out,
    )
    results = pl.pallas_call(
        hand_over,
        out_shape=shapes,
        in_specs=[far] * 7,
        out_specs=[far] * 7,
        scratch_shapes=[pltpu.VMEM(one.shape, one.dtype) for one in shapes] + [pltpu.SemaphoreType.DMA((2, 7))],
        compiler_params=pltpu.CompilerParams(vmem_limit_bytes=58 * 2**20),
    )(*results)
    adapted, fg, gin, gout, *others = results
    return (adapted, fg.T, gin, gout.T, *others)


def solution(mesh):
    return jax.shard_map(
        on_device,
        mesh=mesh,
        in_specs=(
            P("dp", "tensor"),
            P("dp"),
            P(),
            P("dp", "tensor"),
            P("tensor", "dp"),
            P(),
            P("dp", "tensor"),
            P("dp", "tensor"),
        ),
        out_specs=(
            P("dp", "tensor"),
            P("dp", "tensor"),
            P("dp", "tensor"),
            P("tensor", "dp"),
            P("dp", "tensor"),
            P(),
            P(),
        ),
        check_vma=False,
    )
```

```python
import functools

import jax
import jax.numpy as jnp
from jax import lax
from jax.experimental import pallas as pl
from jax.experimental.pallas import tpu as pltpu
from jax.sharding import PartitionSpec as P

EPS = 1e-05
BF = jnp.bfloat16
F32 = jnp.float32
MESH = pl.DeviceIdType.MESH
LANES = 130


def wrap(value, size):
    return lax.rem(value + size, size)


class Place:
    def __init__(self):
        d, t = lax.axis_index("dp"), lax.axis_index("tensor")
        self.t = t
        self.at = {"x": d // 4, "z": d % 4, "y": t // 2, "c": t % 2}

    def shifted(self, axis, delta):
        return wrap(self.at[axis] + delta, 2 if axis == "c" else 4)

    def peer(self, axis, delta):
        if axis == "t":
            return {"tensor": wrap(self.t + delta, 8)}
        place = dict(self.at)
        place[axis] = self.shifted(axis, delta)
        if axis in ("x", "z"):
            return {"dp": place["x"] * 4 + place["z"]}
        return {"tensor": place["y"] * 2 + place["c"]}


class Net:
    def __init__(self, place, sems):
        self.place, self.sems = place, sems
        self.lanes = 0
        self.sent = []

    def lane(self):
        self.lanes += 1
        return self.lanes - 1

    def out_lane(self, gauge):
        lane = self.lane()
        self.sent.append((lane, gauge))
        return lane

    def copy(self, src, dst, axis, delta, out, into):
        pltpu.make_async_remote_copy(
            src_ref=src,
            dst_ref=dst,
            send_sem=self.sems.at[out],
            recv_sem=self.sems.at[into],
            device_id=self.place.peer(axis, delta),
            device_id_type=MESH,
        ).start()

    def whole(self, lane, gauge):
        return pltpu.make_async_remote_copy(
            src_ref=gauge,
            dst_ref=gauge,
            send_sem=self.sems.at[lane],
            recv_sem=self.sems.at[lane],
            device_id=self.place.peer("c", 1),
            device_id_type=MESH,
        )

    def arrived(self, lane, gauge):
        self.whole(lane, gauge).wait_recv()

    def drain(self):
        for lane, gauge in self.sent:
            self.whole(lane, gauge).wait_send()


LOW, HIGH, ALL = pl.ds(0, 48), pl.ds(48, 48), slice(None)
HALVES = (slice(0, 16), slice(16, 32))


class Gather:
    def __init__(self, net, src, buf, half, first, own):
        self.net, self.src, self.buf, self.half, self.own = net, src, buf, half, own
        self.first, self.second = (first, "z" if first == "x" else "x")
        place = net.place
        self.p, self.q = place.at[self.first], place.at[self.second]
        self.out = net.out_lane(buf.at[half, pl.ds(0, 15)])
        self.near, self.far, self.last = net.lane(), net.lane(), net.lane()
        self.waves = [net.lane() for _ in range(3)]

    def slot(self, i, j, rows=ALL):
        return self.buf.at[self.half, i * 4 + j if self.first == "x" else j * 4 + i, rows]

    def wait(self, lane, blocks):
        self.net.arrived(lane, self.buf.at[self.half, pl.ds(0, blocks)])

    def both(self, src, dst, axis, lane):
        for delta in (1, -1):
            self.net.copy(src, dst, axis, delta, self.out, lane)

    def relay(self, slot, axis, lane):
        left, right = self.net.place.shifted(axis, -1), self.net.place.shifted(axis, 1)
        self.net.copy(slot(left, LOW), slot(left, LOW), axis, 1, self.out, lane)
        self.net.copy(slot(right, HIGH), slot(right, HIGH), axis, -1, self.out, lane)

    def ahead(self, delta):
        return self.net.place.shifted(self.first, delta)

    def wave(self, i, lane):
        block = self.slot(i, self.q)
        self.both(block, block, self.second, lane)

    def start(self):
        self.both(self.src, self.slot(self.p, self.q), self.first, self.near)

    def start_across(self):
        self.both(self.src, self.slot(self.p, self.q), self.second, self.waves[0])

    def pass_on(self):
        self.wait(self.near, 2)
        self.relay(lambda i, rows: self.slot(i, self.q, rows), self.first, self.far)
        self.wave(self.ahead(-1), self.waves[1])
        self.wave(self.ahead(1), self.waves[1])

    def turn(self):
        self.wait(self.far, 1)
        self.wave(self.ahead(2), self.waves[2])

    def across(self, i):
        self.relay(lambda j, rows: self.slot(i, j, rows), self.second, self.last)

    def across_own(self):
        self.wait(self.waves[0], 2)
        self.across(self.p)

    def across_next(self):
        self.wait(self.waves[1], 4)
        self.across(self.ahead(-1))
        self.across(self.ahead(1))

    def across_far(self):
        self.wait(self.waves[2], 2)
        self.across(self.ahead(2))

    def finish(self):
        self.wait(self.last, 4)
        self.own.wait()


class Scatter:
    def __init__(self, net, buf, half, first, bufs, gauge, out, out_cols):
        self.net, self.buf, self.half = net, buf, half
        self.first, self.second = (first, "z" if first == "x" else "x")
        self.hop, self.near, self.total, self.last = bufs
        self.out, self.out_cols = out, out_cols
        self.sends = net.out_lane(gauge.at[half, pl.ds(0, 15)])
        self.lanes = [net.lane() for _ in range(3)]

    def group(self, i, rows=ALL):
        if self.first == "x":
            return self.buf.at[self.half, i, :, rows]
        return self.buf.at[self.half, :, i, rows]

    def hop_at(self, side):
        return self.hop.at[self.half, side]

    def near_at(self, side, rows=ALL):
        return self.near.at[self.half, side, :, rows]

    def start(self):
        far, right, left = (self.net.place.shifted(self.first, delta) for delta in (2, 1, -1))
        for part, into, delta, lane in (
            (self.group(far, LOW), self.hop_at(0), 1, 0),
            (self.group(far, HIGH), self.hop_at(1), -1, 0),
            (self.group(right, HIGH), self.near_at(0, HIGH), 1, 1),
            (self.group(left, LOW), self.near_at(1, LOW), -1, 1),
        ):
            self.net.copy(part, into, self.first, delta, self.sends, self.lanes[lane])

    def pass_on(self):
        self.net.arrived(self.lanes[0], self.hop.at[self.half])
        right, left = self.net.place.shifted(self.first, 1), self.net.place.shifted(self.first, -1)
        for side, part, rows, delta in (
            (0, self.group(right, LOW), LOW, 1),
            (1, self.group(left, HIGH), HIGH, -1),
        ):
            part[...] = (part[...].astype(F32) + self.hop_at(side)[...].astype(F32)).astype(BF)
            self.net.copy(part, self.near_at(side, rows), self.first, delta, self.sends, self.lanes[1])

    def turn(self):
        self.net.arrived(self.lanes[1], self.near.at[self.half])
        mine = self.group(self.net.place.at[self.first])
        total = mine[...].astype(F32) + self.near_at(0)[...].astype(F32) + self.near_at(1)[...].astype(F32)
        self.total[self.half] = total.astype(BF)
        for place, delta in enumerate((2, 1, -1)):
            part = self.total.at[self.half, self.net.place.shifted(self.second, delta)]
            self.net.copy(part, self.last.at[self.half, place], self.second, delta, self.sends, self.lanes[2])

    def finish(self):
        self.net.arrived(self.lanes[2], self.last.at[self.half])
        total = self.total[self.half, self.net.place.at[self.second]].astype(F32)
        for place in range(3):
            total = total + self.last[self.half, place].astype(F32)
        self.out[:, self.out_cols] = total


class RowGather:
    def __init__(self, net, buf, rows):
        self.net, self.buf, self.rows = net, buf, rows
        self.c = net.place.at["c"]
        self.out = net.out_lane(self.slots(7))
        self.near, self.far, self.side = net.lane(), net.lane(), net.lane()

    def slots(self, count):
        return self.buf.at[pl.ds(0, count), self.rows]

    def slot(self, delta):
        return self.buf.at[self.net.place.shifted("y", delta) * 2 + self.c, self.rows]

    def beside(self, delta):
        self.net.copy(self.slot(delta), self.slot(delta), "c", 1, self.out, self.side)

    def start(self):
        for delta in (1, -1, 2):
            lane = self.far if delta == 2 else self.near
            self.net.copy(self.slot(0), self.slot(0), "y", delta, self.out, lane)
        self.beside(0)

    def pass_on(self):
        self.net.arrived(self.near, self.slots(2))
        self.beside(-1)
        self.beside(1)
        self.net.arrived(self.far, self.slot(2))
        self.beside(2)

    def finish(self):
        self.net.arrived(self.side, self.slots(4))


class RowScatter:
    def __init__(self, net, bufs):
        self.net = net
        self.part, self.side, self.sums, self.near = bufs
        self.y, self.c = net.place.at["y"], net.place.at["c"]
        self.beside, self.out = net.out_lane(self.side), net.out_lane(self.sums)
        self.one, self.two = net.lane(), [net.lane() for _ in range(2)]

    def put(self, i, value):
        self.part[i] = value.reshape(4, 2, 32, 384)
        self.net.copy(self.part.at[i, :, 1 - self.c], self.side.at[i], "c", 1, self.beside, self.one)

    def pair(self, piece, row):
        rows = HALVES[piece]
        return [self.part[i, row, self.c, rows] + self.side[i, row, rows] for i in range(4)]

    def pass_on(self):
        net = self.net
        net.arrived(self.one, self.side)
        for piece in range(2):
            for place, delta in enumerate((1, -1, 2)):
                for i, value in enumerate(self.pair(piece, net.place.shifted("y", delta))):
                    self.sums[piece, place, :, i * 384 : (i + 1) * 384] = value.astype(BF)
                net.copy(
                    self.sums.at[piece, place], self.near.at[piece, place], "y", delta, self.out, self.two[piece]
                )

    def finish(self, piece):
        total = jnp.concatenate(self.pair(piece, self.y), axis=1)
        self.net.arrived(self.two[piece], self.near.at[piece])
        for place in range(3):
            total = total + self.near[piece, place].astype(F32)
        return total


def row_norm(values):
    center = values - jnp.mean(values, axis=-1, keepdims=True)
    scale = lax.rsqrt(jnp.mean(center * center, axis=-1, keepdims=True) + EPS)
    return (center * scale, scale)


def row_norm_gradient(d_hat, vhat, scale):
    first = jnp.mean(d_hat, axis=-1, keepdims=True)
    second = jnp.mean(d_hat * vhat, axis=-1, keepdims=True)
    return scale * (d_hat - first - vhat * second)


def times(left, right):
    return jnp.dot(left, right, preferred_element_type=F32)


def times_t(left, right):
    return lax.dot_general(left, right, (((1,), (1,)), ((), ())), preferred_element_type=F32)


def kernel(
    frames_in, counts, gain1_in, gain2_in, w_in, w_out, w_ad, grad_out,
    adapted_h, fg_h, gin_h, gout_h, gad_h, gain1_h, gain2_h,
    wi, wo, wa, gi, go, ga,
    hop_i, near_i, tot_i, last_i,
    hop_o, near_o, tot_o, last_o,
    hop_a, near_a, tot_a, last_a,
    adapted_o, fg_o, gin_o, gout_o, gad_o, gain1_o, gain2_o,
    frames, gain1_v, gain2_v, own,
    fr, rows, hid, nrm, dbr, hid_t, nrm_t, dbr_t,
    part_b, side_b, sums_b, near_b,
    part_n, side_n, sums_n, near_n,
    part_h, side_h, sums_h, near_h,
    xhat, yhat, dres, cot, factor, swished, fgs, fgr,
    gn_c, gn_y, gn_x, gn_z,
    sems, local,
):
    place = Place()
    net = Net(place, sems)
    x, z, y, c, t = place.at["x"], place.at["z"], place.at["y"], place.at["c"], place.t

    greeted = [("t", delta) for delta in range(1, 8)] + [(a, delta) for a in "xz" for delta in (1, -1, 2)]
    barrier = pltpu.get_barrier_semaphore()
    for axis, delta in greeted:
        pl.semaphore_signal(barrier, inc=1, device_id=place.peer(axis, delta), device_id_type=MESH)

    loads = []

    def load(src, dst):
        move = pltpu.make_async_copy(src, dst, local.at[len(loads)])
        move.start()
        loads.append(move)
        return move

    frames_load = load(frames_in, frames)
    gain_loads = [load(gain1_in, gain1_v), load(gain2_in, gain2_v)]
    gathers = []
    for src, buf, width in ((w_in, wi, 256), (w_out, wo, 256), (w_ad, wa, 512)):
        for half in range(2):
            cut = src.at[:, pl.ds(half * width, width)]
            gathers.append(Gather(net, cut, buf, half, "xz"[half], load(cut, buf.at[half, x * 4 + z])))
    i0, i1, o0, o1, a0, a1 = gathers
    cot_load = load(grad_out, cot)
    frames_load.wait()
    own[...] = frames[...].T.reshape(8, 32, 192)
    pl.semaphore_wait(barrier, len(greeted))

    def to_peers(src, dst, out, into):
        for delta in range(1, 8):
            net.copy(src.at[wrap(t + delta, 8)], dst.at[t], "t", delta, out, into)

    frames_lane = net.lane()
    to_peers(own, fr, net.out_lane(own.at[pl.ds(0, 7)]), frames_lane)
    for one in (i0, i1):
        one.start()
        one.start_across()
    o0.start()
    o1.start()
    cot_load.wait()
    live = lax.broadcasted_iota(jnp.int32, (256, 1), 0) < counts[0]
    cot[...] = jnp.where(live, cot[...].astype(F32), 0.0).astype(BF)

    fr[t] = own[t]
    for one in gain_loads:
        one.wait()
    gain1, gain2 = gain1_v[...].reshape(1, 1536), gain2_v[...].reshape(1, 1536)
    net.arrived(frames_lane, fr.at[pl.ds(0, 7)])
    for piece in range(8):
        rows[:, piece * 192 : (piece + 1) * 192] = fr[piece].astype(F32)
    normal, rstd1 = row_norm(rows[...])
    xhat[...] = normal
    hid[t] = (normal * gain1).astype(BF)
    hid_rows = RowGather(net, hid, slice(0, 32))
    hid_rows.start()

    i0.pass_on()
    i0.across_own()
    i1.across_own()
    i1.pass_on()
    o0.start_across()
    o1.start_across()
    o0.pass_on()
    o1.pass_on()
    i0.turn()
    i0.across_next()
    i1.turn()
    i1.across_next()
    hid_rows.pass_on()
    o0.across_own()
    o1.across_own()
    o0.turn()
    hid_rows.finish()

    def flat(ref):
        return ref[...].reshape(256, 1536)

    hid_t[...] = flat(hid).T
    o0.across_next()
    o1.turn()
    o1.across_next()
    i0.across_far()
    i1.across_far()
    o0.across_far()
    o1.across_far()
    a1.start()
    a0.start()
    a1.start_across()

    def front(half):
        pre = times(flat(hid), wi[half].reshape(1536, 256))
        sig = jax.nn.sigmoid(pre)
        swished[half] = (pre * sig).astype(BF)
        factor[half] = sig * (1.0 + pre * (1.0 - sig))

    i0.finish()
    front(0)
    i1.finish()
    front(1)
    a0.start_across()
    o0.finish()
    o1.finish()

    def rows_out(scatter, left, weight, look=None):
        for i in range(4):
            some = slice(4 * i, 4 * i + 4)
            value = times_t(left(0), weight[0, some].reshape(384, -1))
            value = value + times_t(left(1), weight[1, some].reshape(384, -1))
            scatter.put(i, value)
            if look is not None:
                look(i, value)

    branch = RowScatter(net, (part_b, side_b, sums_b, near_b))
    rows_out(branch, lambda half: swished[half], wo)
    branch.pass_on()
    a1.pass_on()
    a0.pass_on()
    a0.across_own()
    a1.across_own()

    rstd2 = []
    nrm_rows = [RowGather(net, nrm, piece) for piece in HALVES]

    def middle(piece):
        half = HALVES[piece]
        normal, scale = row_norm(rows[half] + 0.5 * branch.finish(piece))
        rstd2.append(scale)
        yhat[half] = normal
        nrm[t, half] = (normal * gain2).astype(BF)
        nrm_rows[piece].start()

    middle(0)
    a1.turn()
    middle(1)
    a0.turn()
    a1.across_next()
    nrm_rows[0].pass_on()
    a0.across_next()
    nrm_rows[1].pass_on()
    a1.across_far()
    a0.across_far()
    nrm_rows[0].finish()
    nrm_rows[1].finish()

    def outer(grad, half, left, right):
        def body(i, carry):
            some = left[pl.ds(pl.multiple_of(i * 384, 128), 384), :]
            grad[half, i] = times(some, right).astype(BF).reshape(4, 96, -1)
            return carry

        lax.fori_loop(0, 4, body, 0)

    def scatter(buf, bufs, gauge, out, width):
        return [
            Scatter(net, buf, half, "zx"[half], bufs, gauge, out, pl.ds(half * width, width))
            for half in range(2)
        ]

    sa0, sa1 = scatter(ga, (hop_a, near_a, tot_a, last_a), wa, gad_o, 512)
    so0, so1 = scatter(go, (hop_o, near_o, tot_o, last_o), wo, gout_o, 256)
    si0, si1 = scatter(gi, (hop_i, near_i, tot_i, last_i), wi, gin_o, 256)

    nrm_t[...] = flat(nrm).T
    outer(ga, 0, nrm_t, cot[:, :512])
    sa0.start()
    outer(ga, 1, nrm_t, cot[:, 512:])
    sa1.start()

    a0.finish()
    a1.finish()
    d_norm = RowScatter(net, (part_n, side_n, sums_n, near_n))
    rows_out(d_norm, lambda half: cot[:, half * 512 : (half + 1) * 512], wa)

    def adapt(half):
        value = times(flat(nrm), wa[half].reshape(1536, 512))
        adapted_o[:, half * 512 : (half + 1) * 512] = jnp.where(live, value, 0.0).astype(BF)

    adapt(0)
    d_norm.pass_on()
    adapt(1)
    stores = [load(adapted_o, adapted_h)]
    sa0.pass_on()
    sa1.pass_on()

    gain2_parts = []
    dbr_rows = [RowGather(net, dbr, piece) for piece in HALVES]

    def back(piece):
        half = HALVES[piece]
        d_normed, normal = d_norm.finish(piece), yhat[half]
        gain2_parts.append(jnp.sum(d_normed * normal, axis=0, keepdims=True))
        d_resid = row_norm_gradient(d_normed * gain2, normal, rstd2[piece])
        dres[half] = d_resid
        dbr[t, half] = (0.5 * d_resid).astype(BF)
        dbr_rows[piece].start()

    back(0)
    back(1)
    dbr_rows[0].pass_on()
    sa0.turn()
    dbr_rows[0].finish()
    dbr_rows[1].pass_on()
    sa1.turn()
    dbr_rows[1].finish()

    pres = []

    def before(half):
        d_swished = times(flat(dbr), wo[half].reshape(1536, 256))
        pres.append((d_swished * factor[half]).astype(BF))

    def gain_start(buf, axis, total):
        here = buf.at[place.at[axis]]
        here[...] = total
        out, into = net.out_lane(buf.at[pl.ds(0, 3)]), net.lane()
        for delta in (1, -1, 2):
            net.copy(here, here, axis, delta, out, into)
        return into

    def gain_sum(into, buf):
        net.arrived(into, buf.at[pl.ds(0, 3)])
        return buf[0] + buf[1] + buf[2] + buf[3]

    dbr_t[...] = flat(dbr).T
    outer(go, 0, dbr_t, swished[0])
    so0.start()
    outer(go, 1, dbr_t, swished[1])
    so1.start()
    before(0)
    before(1)
    d_hid = RowScatter(net, (part_h, side_h, sums_h, near_h))
    gain1_sums = []

    def look(i, value):
        some = hid[:, :, i * 384 : (i + 1) * 384].reshape(256, 384).astype(F32)
        gain1_sums.append(jnp.sum(value * some, axis=0, keepdims=True))

    rows_out(d_hid, lambda half: pres[half], wi, look)
    gain1_part = jnp.concatenate(gain1_sums, axis=1) / gain1
    gn_c[c] = jnp.concatenate([gain1_part, gain2_parts[0] + gain2_parts[1]], axis=0)
    lane = net.lane()
    net.copy(gn_c.at[c], gn_c.at[c], "c", 1, net.out_lane(gn_c.at[0]), lane)

    outer(gi, 0, hid_t, pres[0])
    si0.start()
    d_hid.pass_on()
    outer(gi, 1, hid_t, pres[1])
    si1.start()
    net.arrived(lane, gn_c.at[1 - c])
    lane = gain_start(gn_y, "y", gn_c[0] + gn_c[1])
    so0.pass_on()
    so1.pass_on()
    lane = gain_start(gn_x, "x", gain_sum(lane, gn_y))
    si0.pass_on()
    si1.pass_on()

    d_hidden = jnp.concatenate([d_hid.finish(0), d_hid.finish(1)], axis=0)
    grad_rows = dres[...] + row_norm_gradient(d_hidden * gain1, xhat[...], rstd1)
    for piece in range(8):
        fgs[piece] = grad_rows[:, piece * 192 : (piece + 1) * 192]
    fgr[t] = fgs[t]
    rows_lane = net.lane()
    to_peers(fgs, fgr, net.out_lane(fgs.at[pl.ds(0, 7)]), rows_lane)
    sa1.finish()
    sa0.finish()
    stores.append(load(gad_o, gad_h))
    lane = gain_start(gn_z, "z", gain_sum(lane, gn_x))
    so0.turn()
    so1.turn()
    net.arrived(rows_lane, fgr.at[pl.ds(0, 7)])
    fg_o[...] = fgr[...].reshape(256, 192).T
    stores.append(load(fg_o, fg_h))
    si0.turn()
    si1.turn()
    total = gain_sum(lane, gn_z)
    gain1_o[...] = total[0]
    gain2_o[...] = total[1]
    stores.append(load(gain1_o, gain1_h))
    stores.append(load(gain2_o, gain2_h))
    so0.finish()
    so1.finish()
    stores.append(load(gout_o, gout_h))
    si0.finish()
    si1.finish()
    stores.append(load(gin_o, gin_h))
    net.drain()
    for move in stores:
        move.wait()


def hand_over(*refs):
    count = len(refs) // 3
    sems = refs[-1]
    moves = []
    for i in range(count):
        hold = refs[2 * count + i]
        moves.append(
            (
                pltpu.make_async_copy(refs[i], hold, sems.at[0, i]),
                pltpu.make_async_copy(hold, refs[count + i], sems.at[1, i]),
            )
        )
        moves[-1][0].start()
    for come, go in moves:
        come.wait()
        go.start()
    for come, go in moves:
        go.wait()


def on_device(frames, counts, layer_norm_gain1, w_in, w_out, norm_gain2, w_adapt, grad_out):
    def weight(width):
        return pltpu.VMEM((2, 16, 96, width), BF)

    def gradient(width):
        return pltpu.VMEM((2, 4, 4, 96, width), BF)

    def sums(width):
        return [
            pltpu.VMEM((2, 2, 4, 48, width), BF),
            pltpu.VMEM((2, 2, 4, 96, width), BF),
            pltpu.VMEM((2, 4, 96, width), BF),
            pltpu.VMEM((2, 3, 96, width), BF),
        ]

    shape = jax.ShapeDtypeStruct
    shapes = (
        shape((256, 1024), BF),
        shape((192, 256), F32),
        shape((96, 512), F32),
        shape((96, 512), F32),
        shape((96, 1024), F32),
        shape((1536,), F32),
        shape((1536,), F32),
    )
    slots = pltpu.VMEM((8, 32, 1536), BF)
    row_sums = [
        pltpu.VMEM((4, 4, 2, 32, 384), F32),
        pltpu.VMEM((4, 4, 32, 384), F32),
        pltpu.VMEM((2, 3, 16, 1536), BF),
        pltpu.VMEM((2, 3, 16, 1536), BF),
    ]
    scratch = (
        [weight(256), weight(256), weight(512), gradient(256), gradient(256), gradient(512)]
        + sums(256)
        + sums(256)
        + sums(512)
        + [pltpu.VMEM(one.shape, one.dtype) for one in shapes]
        + [pltpu.VMEM((192, 256), BF), pltpu.VMEM((1536,), F32), pltpu.VMEM((1536,), F32)]
        + [pltpu.VMEM((8, 32, 192), BF)]
        + [pltpu.VMEM((8, 32, 192), BF), pltpu.VMEM((32, 1536), F32)]
        + [slots] * 3
        + [pltpu.VMEM((1536, 256), BF)] * 3
        + row_sums * 3
        + [pltpu.VMEM((32, 1536), F32)] * 3
        + [pltpu.VMEM((256, 1024), BF)]
        + [pltpu.VMEM((2, 256, 256), F32), pltpu.VMEM((2, 256, 256), BF)]
        + [pltpu.VMEM((8, 32, 192), F32)] * 2
        + [pltpu.VMEM((2, 2, 1536), F32)]
        + [pltpu.VMEM((4, 2, 1536), F32)] * 3
        + [pltpu.SemaphoreType.DMA((LANES,)), pltpu.SemaphoreType.DMA((17,))]
    )
    far = pl.BlockSpec(memory_space=pl.ANY)
    results = pl.pallas_call(
        kernel,
        out_shape=shapes,
        in_specs=[far, pl.BlockSpec(memory_space=pltpu.SMEM)] + [far] * 6,
        out_specs=[far] * 7,
        scratch_shapes=scratch,
        compiler_params=pltpu.CompilerParams(
            collective_id=0, has_side_effects=True, vmem_limit_bytes=58 * 2**20
        ),
    )(
        frames.T,
        counts,
        layer_norm_gain1,
        norm_gain2,
        w_in,
        w_out.T,
        w_adapt,
        grad_out,
    )
    results = pl.pallas_call(
        hand_over,
        out_shape=shapes,
        in_specs=[far] * 7,
        out_specs=[far] * 7,
        scratch_shapes=[pltpu.VMEM(one.shape, one.dtype) for one in shapes] + [pltpu.SemaphoreType.DMA((2, 7))],
        compiler_params=pltpu.CompilerParams(vmem_limit_bytes=58 * 2**20),
    )(*results)
    adapted, fg, gin, gout, *others = results
    return (adapted, fg.T, gin, gout.T, *others)


def solution(mesh):
    return jax.shard_map(
        on_device,
        mesh=mesh,
        in_specs=(
            P("dp", "tensor"),
            P("dp"),
            P(),
            P("dp", "tensor"),
            P("tensor", "dp"),
            P(),
            P("dp", "tensor"),
            P("dp", "tensor"),
        ),
        out_specs=(
            P("dp", "tensor"),
            P("dp", "tensor"),
            P("dp", "tensor"),
            P("tensor", "dp"),
            P("dp", "tensor"),
            P(),
            P(),
        ),
        check_vma=False,
    )
```

```python
import functools

import jax
import jax.numpy as jnp
from jax import lax
from jax.experimental import pallas as pl
from jax.experimental.pallas import tpu as pltpu
from jax.sharding import PartitionSpec as P

EPS = 1e-05
BF = jnp.bfloat16
F32 = jnp.float32
MESH = pl.DeviceIdType.MESH
LANES = 113


def wrap(value, size):
    return lax.rem(value + size, size)


class Place:
    def __init__(self):
        d, t = lax.axis_index("dp"), lax.axis_index("tensor")
        self.t = t
        self.at = {"x": d // 4, "z": d % 4, "y": t // 2, "c": t % 2}

    def shifted(self, axis, delta):
        return wrap(self.at[axis] + delta, 2 if axis == "c" else 4)

    def peer(self, axis, delta):
        if axis == "t":
            return {"tensor": wrap(self.t + delta, 8)}
        place = dict(self.at)
        place[axis] = self.shifted(axis, delta)
        if axis in ("x", "z"):
            return {"dp": place["x"] * 4 + place["z"]}
        return {"tensor": place["y"] * 2 + place["c"]}


class Net:
    def __init__(self, place, sems):
        self.place, self.sems = place, sems
        self.lanes = 0
        self.sent = []

    def lane(self):
        self.lanes += 1
        return self.lanes - 1

    def out_lane(self, gauge):
        lane = self.lane()
        self.sent.append((lane, gauge))
        return lane

    def copy(self, src, dst, axis, delta, out, into):
        pltpu.make_async_remote_copy(
            src_ref=src,
            dst_ref=dst,
            send_sem=self.sems.at[out],
            recv_sem=self.sems.at[into],
            device_id=self.place.peer(axis, delta),
            device_id_type=MESH,
        ).start()

    def whole(self, lane, gauge):
        return pltpu.make_async_remote_copy(
            src_ref=gauge,
            dst_ref=gauge,
            send_sem=self.sems.at[lane],
            recv_sem=self.sems.at[lane],
            device_id=self.place.peer("c", 1),
            device_id_type=MESH,
        )

    def arrived(self, lane, gauge):
        self.whole(lane, gauge).wait_recv()

    def drain(self):
        for lane, gauge in self.sent:
            self.whole(lane, gauge).wait_send()


LOW, HIGH, ALL = pl.ds(0, 48), pl.ds(48, 48), slice(None)
HALVES = (slice(0, 16), slice(16, 32))


class Gather:
    def __init__(self, net, src, buf, half, first, own):
        self.net, self.src, self.buf, self.half, self.own = net, src, buf, half, own
        self.first, self.second = (first, "z" if first == "x" else "x")
        place = net.place
        self.p, self.q = place.at[self.first], place.at[self.second]
        self.out = net.out_lane(buf.at[half, pl.ds(0, 15)])
        self.near, self.far, self.last = net.lane(), net.lane(), net.lane()
        self.waves = [net.lane() for _ in range(3)]

    def slot(self, i, j, rows=ALL):
        return self.buf.at[self.half, i * 4 + j if self.first == "x" else j * 4 + i, rows]

    def wait(self, lane, blocks):
        self.net.arrived(lane, self.buf.at[self.half, pl.ds(0, blocks)])

    def both(self, src, dst, axis, lane):
        for delta in (1, -1):
            self.net.copy(src, dst, axis, delta, self.out, lane)

    def relay(self, slot, axis, lane):
        left, right = self.net.place.shifted(axis, -1), self.net.place.shifted(axis, 1)
        self.net.copy(slot(left, LOW), slot(left, LOW), axis, 1, self.out, lane)
        self.net.copy(slot(right, HIGH), slot(right, HIGH), axis, -1, self.out, lane)

    def ahead(self, delta):
        return self.net.place.shifted(self.first, delta)

    def wave(self, i, lane):
        block = self.slot(i, self.q)
        self.both(block, block, self.second, lane)

    def start(self):
        self.both(self.src, self.slot(self.p, self.q), self.first, self.near)

    def start_across(self):
        self.both(self.src, self.slot(self.p, self.q), self.second, self.waves[0])

    def pass_on(self):
        self.wait(self.near, 2)
        self.relay(lambda i, rows: self.slot(i, self.q, rows), self.first, self.far)
        self.wave(self.ahead(-1), self.waves[1])
        self.wave(self.ahead(1), self.waves[1])

    def turn(self):
        self.wait(self.far, 1)
        self.wave(self.ahead(2), self.waves[2])

    def across(self, i):
        self.relay(lambda j, rows: self.slot(i, j, rows), self.second, self.last)

    def across_own(self):
        self.wait(self.waves[0], 2)
        self.across(self.p)

    def across_next(self):
        self.wait(self.waves[1], 4)
        self.across(self.ahead(-1))
        self.across(self.ahead(1))

    def across_far(self):
        self.wait(self.waves[2], 2)
        self.across(self.ahead(2))

    def finish(self):
        self.wait(self.last, 4)
        self.own.wait()


class Scatter:
    def __init__(self, net, buf, half, first, bufs, gauge, out, out_cols):
        self.net, self.buf, self.half = net, buf, half
        self.first, self.second = (first, "z" if first == "x" else "x")
        self.hop, self.near, self.total, self.last = bufs
        self.out, self.out_cols = out, out_cols
        self.sends = net.out_lane(gauge.at[half, pl.ds(0, 15)])
        self.lanes = [net.lane() for _ in range(3)]

    def group(self, i, rows=ALL):
        if self.first == "x":
            return self.buf.at[self.half, i, :, rows]
        return self.buf.at[self.half, :, i, rows]

    def hop_at(self, side):
        return self.hop.at[self.half, side]

    def near_at(self, side, rows=ALL):
        return self.near.at[self.half, side, :, rows]

    def start(self):
        far, right, left = (self.net.place.shifted(self.first, delta) for delta in (2, 1, -1))
        for part, into, delta, lane in (
            (self.group(far, LOW), self.hop_at(0), 1, 0),
            (self.group(far, HIGH), self.hop_at(1), -1, 0),
            (self.group(right, HIGH), self.near_at(0, HIGH), 1, 1),
            (self.group(left, LOW), self.near_at(1, LOW), -1, 1),
        ):
            self.net.copy(part, into, self.first, delta, self.sends, self.lanes[lane])

    def pass_on(self):
        self.net.arrived(self.lanes[0], self.hop.at[self.half])
        right, left = self.net.place.shifted(self.first, 1), self.net.place.shifted(self.first, -1)
        for side, part, rows, delta in (
            (0, self.group(right, LOW), LOW, 1),
            (1, self.group(left, HIGH), HIGH, -1),
        ):
            part[...] = (part[...].astype(F32) + self.hop_at(side)[...].astype(F32)).astype(BF)
            self.net.copy(part, self.near_at(side, rows), self.first, delta, self.sends, self.lanes[1])

    def turn(self):
        self.net.arrived(self.lanes[1], self.near.at[self.half])
        mine = self.group(self.net.place.at[self.first])
        total = mine[...].astype(F32) + self.near_at(0)[...].astype(F32) + self.near_at(1)[...].astype(F32)
        self.total[self.half] = total.astype(BF)
        for place, delta in enumerate((2, 1, -1)):
            part = self.total.at[self.half, self.net.place.shifted(self.second, delta)]
            self.net.copy(part, self.last.at[self.half, place], self.second, delta, self.sends, self.lanes[2])

    def finish(self):
        self.net.arrived(self.lanes[2], self.last.at[self.half])
        total = self.total[self.half, self.net.place.at[self.second]].astype(F32)
        for place in range(3):
            total = total + self.last[self.half, place].astype(F32)
        self.out[:, self.out_cols] = total


class RowGather:
    def __init__(self, net, buf, rows):
        self.net, self.buf, self.rows = net, buf, rows
        self.c = net.place.at["c"]
        self.out = net.out_lane(self.slots(7))
        self.near, self.far, self.side = net.lane(), net.lane(), net.lane()

    def slots(self, count):
        return self.buf.at[pl.ds(0, count), self.rows]

    def slot(self, delta):
        return self.buf.at[self.net.place.shifted("y", delta) * 2 + self.c, self.rows]

    def beside(self, delta):
        self.net.copy(self.slot(delta), self.slot(delta), "c", 1, self.out, self.side)

    def start(self):
        for delta in (1, -1, 2):
            lane = self.far if delta == 2 else self.near
            self.net.copy(self.slot(0), self.slot(0), "y", delta, self.out, lane)
        self.beside(0)

    def pass_on(self):
        self.net.arrived(self.near, self.slots(2))
        self.beside(-1)
        self.beside(1)
        self.net.arrived(self.far, self.slot(2))
        self.beside(2)

    def finish(self):
        self.net.arrived(self.side, self.slots(4))


class RowScatter:
    def __init__(self, net, bufs):
        self.net = net
        self.part, self.side, self.sums, self.near = bufs
        self.y, self.c = net.place.at["y"], net.place.at["c"]
        self.beside, self.out = net.out_lane(self.side), net.out_lane(self.sums)
        self.one, self.two = net.lane(), [net.lane() for _ in range(2)]

    def put(self, i, value):
        self.part[i] = value.reshape(4, 2, 32, 384)
        self.net.copy(self.part.at[i, :, 1 - self.c], self.side.at[i], "c", 1, self.beside, self.one)

    def pair(self, piece, row):
        rows = HALVES[piece]
        return [self.part[i, row, self.c, rows] + self.side[i, row, rows] for i in range(4)]

    def pass_on(self):
        net = self.net
        net.arrived(self.one, self.side)
        for piece in range(2):
            for place, delta in enumerate((1, -1, 2)):
                for i, value in enumerate(self.pair(piece, net.place.shifted("y", delta))):
                    self.sums[piece, place, :, i * 384 : (i + 1) * 384] = value.astype(BF)
                net.copy(
                    self.sums.at[piece, place], self.near.at[piece, place], "y", delta, self.out, self.two[piece]
                )

    def finish(self, piece):
        total = jnp.concatenate(self.pair(piece, self.y), axis=1)
        self.net.arrived(self.two[piece], self.near.at[piece])
        for place in range(3):
            total = total + self.near[piece, place].astype(F32)
        return total


def row_norm(values):
    center = values - jnp.mean(values, axis=-1, keepdims=True)
    scale = lax.rsqrt(jnp.mean(center * center, axis=-1, keepdims=True) + EPS)
    return (center * scale, scale)


def row_norm_gradient(d_hat, vhat, scale):
    first = jnp.mean(d_hat, axis=-1, keepdims=True)
    second = jnp.mean(d_hat * vhat, axis=-1, keepdims=True)
    return scale * (d_hat - first - vhat * second)


def times(left, right):
    return jnp.dot(left, right, preferred_element_type=F32)


def times_t(left, right):
    return lax.dot_general(left, right, (((1,), (1,)), ((), ())), preferred_element_type=F32)


def kernel(
    frames_in, counts_in, gain1_in, gain2_in, w_in, w_out, w_ad, grad_out,
    adapted_h, fg_h, gin_h, gout_h, gad_h, gain1_h, gain2_h,
    wi, wo, wa, gi, go, ga,
    hop_i, near_i, tot_i, last_i,
    hop_o, near_o, tot_o, last_o,
    hop_a, near_a, tot_a, last_a,
    adapted_o, fg_o, gin_o, gout_o, gad_o, gain1_o, gain2_o,
    counts, frames, gain1_v, gain2_v, own,
    fr, rows, hid, nrm, dbr, hid_t, nrm_t, dbr_t,
    part_b, side_b, sums_b, near_b,
    part_n, side_n, sums_n, near_n,
    part_h, side_h, sums_h, near_h,
    xhat, yhat, dres, cot, factor, swished, fgs, fgr,
    gn_c, gn_y, gn_x, gn_z,
    sems, local,
):
    place = Place()
    net = Net(place, sems)
    x, z, y, c, t = place.at["x"], place.at["z"], place.at["y"], place.at["c"], place.t

    greeted = [("t", delta) for delta in range(1, 8)] + [(a, delta) for a in "xz" for delta in (1, -1, 2)]
    barrier = pltpu.get_barrier_semaphore()
    for axis, delta in greeted:
        pl.semaphore_signal(barrier, inc=1, device_id=place.peer(axis, delta), device_id_type=MESH)

    loads = []

    def load(src, dst):
        move = pltpu.make_async_copy(src, dst, local.at[len(loads)])
        move.start()
        loads.append(move)
        return move

    frames_load = load(frames_in, frames)
    gain_loads = [load(gain1_in, gain1_v), load(gain2_in, gain2_v)]
    gathers = []
    for src, buf, width in ((w_in, wi, 256), (w_out, wo, 256), (w_ad, wa, 512)):
        for half in range(2):
            cut = src.at[:, pl.ds(half * width, width)]
            gathers.append(Gather(net, cut, buf, half, "xz"[half], load(cut, buf.at[half, x * 4 + z])))
    i0, i1, o0, o1, a0, a1 = gathers
    cot_load = load(grad_out, cot)
    counts_load = load(counts_in, counts)
    frames_load.wait()
    own[...] = frames[...].T.reshape(8, 32, 192)
    pl.semaphore_wait(barrier, len(greeted))

    def to_peers(src, dst, out, into):
        for delta in range(1, 8):
            net.copy(src.at[wrap(t + delta, 8)], dst.at[t], "t", delta, out, into)

    frames_lane = net.lane()
    to_peers(own, fr, net.out_lane(own.at[pl.ds(0, 7)]), frames_lane)
    for one in (i0, i1):
        one.start()
        one.start_across()
    o0.start()
    o1.start()
    cot_load.wait()
    counts_load.wait()
    live = lax.broadcasted_iota(jnp.int32, (256, 1), 0) < counts[0]
    cot[...] = jnp.where(live, cot[...].astype(F32), 0.0).astype(BF)

    fr[t] = own[t]
    for one in gain_loads:
        one.wait()
    gain1, gain2 = gain1_v[...].reshape(1, 1536), gain2_v[...].reshape(1, 1536)
    net.arrived(frames_lane, fr.at[pl.ds(0, 7)])
    for piece in range(8):
        rows[:, piece * 192 : (piece + 1) * 192] = fr[piece].astype(F32)
    normal, rstd1 = row_norm(rows[...])
    xhat[...] = normal
    hid[t] = (normal * gain1).astype(BF)
    hid_rows = RowGather(net, hid, slice(0, 32))
    hid_rows.start()

    i0.pass_on()
    i0.across_own()
    i1.across_own()
    i1.pass_on()
    o0.start_across()
    o1.start_across()
    o0.pass_on()
    o1.pass_on()
    i0.turn()
    i0.across_next()
    i1.turn()
    i1.across_next()
    hid_rows.pass_on()
    o0.across_own()
    o1.across_own()
    o0.turn()
    hid_rows.finish()

    def flat(ref):
        return ref[...].reshape(256, 1536)

    hid_t[...] = flat(hid).T
    o0.across_next()
    o1.turn()
    o1.across_next()
    i0.across_far()
    i1.across_far()
    o0.across_far()
    o1.across_far()
    a1.start()
    a0.start()
    a1.start_across()

    def front(half):
        pre = times(flat(hid), wi[half].reshape(1536, 256))
        sig = jax.nn.sigmoid(pre)
        swished[half] = (pre * sig).astype(BF)
        factor[half] = sig * (1.0 + pre * (1.0 - sig))

    i0.finish()
    front(0)
    i1.finish()
    front(1)
    a0.start_across()
    o0.finish()
    o1.finish()

    def rows_out(scatter, left, weight, look=None):
        for i in range(4):
            some = slice(4 * i, 4 * i + 4)
            value = times_t(left(0), weight[0, some].reshape(384, -1))
            value = value + times_t(left(1), weight[1, some].reshape(384, -1))
            scatter.put(i, value)
            if look is not None:
                look(i, value)

    branch = RowScatter(net, (part_b, side_b, sums_b, near_b))
    rows_out(branch, lambda half: swished[half], wo)
    branch.pass_on()
    a1.pass_on()
    a0.pass_on()
    a0.across_own()
    a1.across_own()

    rstd2 = []
    nrm_rows = [RowGather(net, nrm, piece) for piece in HALVES]

    def middle(piece):
        half = HALVES[piece]
        normal, scale = row_norm(rows[half] + 0.5 * branch.finish(piece))
        rstd2.append(scale)
        yhat[half] = normal
        nrm[t, half] = (normal * gain2).astype(BF)
        nrm_rows[piece].start()

    middle(0)
    a1.turn()
    middle(1)
    a0.turn()
    a1.across_next()
    nrm_rows[0].pass_on()
    a0.across_next()
    nrm_rows[1].pass_on()
    a1.across_far()
    a0.across_far()
    nrm_rows[0].finish()
    nrm_rows[1].finish()

    def outer(grad, half, left, right):
        def body(i, carry):
            some = left[pl.ds(pl.multiple_of(i * 384, 128), 384), :]
            grad[half, i] = times(some, right).astype(BF).reshape(4, 96, -1)
            return carry

        lax.fori_loop(0, 4, body, 0)

    def scatter(buf, bufs, gauge, out, width):
        return [
            Scatter(net, buf, half, "zx"[half], bufs, gauge, out, pl.ds(half * width, width))
            for half in range(2)
        ]

    sa0, sa1 = scatter(ga, (hop_a, near_a, tot_a, last_a), wa, gad_o, 512)
    so0, so1 = scatter(go, (hop_o, near_o, tot_o, last_o), wo, gout_o, 256)
    si0, si1 = scatter(gi, (hop_i, near_i, tot_i, last_i), wi, gin_o, 256)

    nrm_t[...] = flat(nrm).T
    outer(ga, 0, nrm_t, cot[:, :512])
    sa0.start()
    outer(ga, 1, nrm_t, cot[:, 512:])
    sa1.start()

    a0.finish()
    a1.finish()
    d_norm = RowScatter(net, (part_n, side_n, sums_n, near_n))
    rows_out(d_norm, lambda half: cot[:, half * 512 : (half + 1) * 512], wa)

    def adapt(half):
        value = times(flat(nrm), wa[half].reshape(1536, 512))
        adapted_o[:, half * 512 : (half + 1) * 512] = jnp.where(live, value, 0.0).astype(BF)

    adapt(0)
    d_norm.pass_on()
    adapt(1)
    stores = [load(adapted_o, adapted_h)]
    sa0.pass_on()
    sa1.pass_on()

    gain2_parts = []
    dbr_rows = [RowGather(net, dbr, piece) for piece in HALVES]

    def back(piece):
        half = HALVES[piece]
        d_normed, normal = d_norm.finish(piece), yhat[half]
        gain2_parts.append(jnp.sum(d_normed * normal, axis=0, keepdims=True))
        d_resid = row_norm_gradient(d_normed * gain2, normal, rstd2[piece])
        dres[half] = d_resid
        dbr[t, half] = (0.5 * d_resid).astype(BF)
        dbr_rows[piece].start()

    back(0)
    back(1)
    dbr_rows[0].pass_on()
    sa0.turn()
    dbr_rows[0].finish()
    dbr_rows[1].pass_on()
    sa1.turn()
    dbr_rows[1].finish()

    pres = []

    def before(half):
        d_swished = times(flat(dbr), wo[half].reshape(1536, 256))
        pres.append((d_swished * factor[half]).astype(BF))

    def gain_start(buf, axis, total):
        here = buf.at[place.at[axis]]
        here[...] = total
        out, into = net.out_lane(buf.at[pl.ds(0, 3)]), net.lane()
        for delta in (1, -1, 2):
            net.copy(here, here, axis, delta, out, into)
        return into

    def gain_sum(into, buf):
        net.arrived(into, buf.at[pl.ds(0, 3)])
        return buf[0] + buf[1] + buf[2] + buf[3]

    dbr_t[...] = flat(dbr).T
    outer(go, 0, dbr_t, swished[0])
    so0.start()
    outer(go, 1, dbr_t, swished[1])
    so1.start()
    before(0)
    before(1)
    d_hid = RowScatter(net, (part_h, side_h, sums_h, near_h))
    gain1_sums = []

    def look(i, value):
        some = hid[:, :, i * 384 : (i + 1) * 384].reshape(256, 384).astype(F32)
        gain1_sums.append(jnp.sum(value * some, axis=0, keepdims=True))

    rows_out(d_hid, lambda half: pres[half], wi, look)
    gain1_part = jnp.concatenate(gain1_sums, axis=1) / gain1
    gn_c[c] = jnp.concatenate([gain1_part, gain2_parts[0] + gain2_parts[1]], axis=0)
    lane = net.lane()
    net.copy(gn_c.at[c], gn_c.at[c], "c", 1, net.out_lane(gn_c.at[0]), lane)

    outer(gi, 0, hid_t, pres[0])
    si0.start()
    d_hid.pass_on()
    outer(gi, 1, hid_t, pres[1])
    si1.start()
    net.arrived(lane, gn_c.at[1 - c])
    lane = gain_start(gn_y, "y", gn_c[0] + gn_c[1])
    so0.pass_on()
    so1.pass_on()
    lane = gain_start(gn_x, "x", gain_sum(lane, gn_y))
    si0.pass_on()
    si1.pass_on()

    d_hidden = jnp.concatenate([d_hid.finish(0), d_hid.finish(1)], axis=0)
    grad_rows = dres[...] + row_norm_gradient(d_hidden * gain1, xhat[...], rstd1)
    for piece in range(8):
        fgs[piece] = grad_rows[:, piece * 192 : (piece + 1) * 192]
    fgr[t] = fgs[t]
    rows_lane = net.lane()
    to_peers(fgs, fgr, net.out_lane(fgs.at[pl.ds(0, 7)]), rows_lane)
    sa1.finish()
    sa0.finish()
    stores.append(load(gad_o, gad_h))
    lane = gain_start(gn_z, "z", gain_sum(lane, gn_x))
    so0.turn()
    so1.turn()
    net.arrived(rows_lane, fgr.at[pl.ds(0, 7)])
    fg_o[...] = fgr[...].reshape(256, 192).T
    stores.append(load(fg_o, fg_h))
    si0.turn()
    si1.turn()
    total = gain_sum(lane, gn_z)
    gain1_o[...] = total[0]
    gain2_o[...] = total[1]
    stores.append(load(gain1_o, gain1_h))
    stores.append(load(gain2_o, gain2_h))
    so0.finish()
    so1.finish()
    stores.append(load(gout_o, gout_h))
    si0.finish()
    si1.finish()
    stores.append(load(gin_o, gin_h))
    net.drain()
    for move in stores:
        move.wait()


def hand_over(*refs):
    count = len(refs) // 3
    sems = refs[-1]
    moves = []
    for i in range(count):
        hold = refs[2 * count + i]
        moves.append(
            (
                pltpu.make_async_copy(refs[i], hold, sems.at[0, i]),
                pltpu.make_async_copy(hold, refs[count + i], sems.at[1, i]),
            )
        )
        moves[-1][0].start()
    for come, go in moves:
        come.wait()
        go.start()
    for come, go in moves:
        go.wait()


def on_device(frames, counts, layer_norm_gain1, w_in, w_out, norm_gain2, w_adapt, grad_out):
    def weight(width):
        return pltpu.VMEM((2, 16, 96, width), BF)

    def gradient(width):
        return pltpu.VMEM((2, 4, 4, 96, width), BF)

    def sums(width):
        return [
            pltpu.VMEM((2, 2, 4, 48, width), BF),
            pltpu.VMEM((2, 2, 4, 96, width), BF),
            pltpu.VMEM((2, 4, 96, width), BF),
            pltpu.VMEM((2, 3, 96, width), BF),
        ]

    shape = jax.ShapeDtypeStruct
    shapes = (
        shape((256, 1024), BF),
        shape((192, 256), F32),
        shape((96, 512), F32),
        shape((96, 512), F32),
        shape((96, 1024), F32),
        shape((1536,), F32),
        shape((1536,), F32),
    )
    slots = pltpu.VMEM((8, 32, 1536), BF)
    row_sums = [
        pltpu.VMEM((4, 4, 2, 32, 384), F32),
        pltpu.VMEM((4, 4, 32, 384), F32),
        pltpu.VMEM((2, 3, 16, 1536), BF),
        pltpu.VMEM((2, 3, 16, 1536), BF),
    ]
    scratch = (
        [weight(256), weight(256), weight(512), gradient(256), gradient(256), gradient(512)]
        + sums(256)
        + sums(256)
        + sums(512)
        + [pltpu.VMEM(one.shape, one.dtype) for one in shapes]
        + [pltpu.SMEM((1,), jnp.int32), pltpu.VMEM((192, 256), BF), pltpu.VMEM((1536,), F32), pltpu.VMEM((1536,), F32)]
        + [pltpu.VMEM((8, 32, 192), BF)]
        + [pltpu.VMEM((8, 32, 192), BF), pltpu.VMEM((32, 1536), F32)]
        + [slots] * 3
        + [pltpu.VMEM((1536, 256), BF)] * 3
        + row_sums * 3
        + [pltpu.VMEM((32, 1536), F32)] * 3
        + [pltpu.VMEM((256, 1024), BF)]
        + [pltpu.VMEM((2, 256, 256), F32), pltpu.VMEM((2, 256, 256), BF)]
        + [pltpu.VMEM((8, 32, 192), F32)] * 2
        + [pltpu.VMEM((2, 2, 1536), F32)]
        + [pltpu.VMEM((4, 2, 1536), F32)] * 3
        + [pltpu.SemaphoreType.DMA((LANES,)), pltpu.SemaphoreType.DMA((18,))]
    )
    far = pl.BlockSpec(memory_space=pl.ANY)
    results = pl.pallas_call(
        kernel,
        out_shape=shapes,
        in_specs=[far] * 8,
        out_specs=[far] * 7,
        scratch_shapes=scratch,
        compiler_params=pltpu.CompilerParams(
            collective_id=0, has_side_effects=True, vmem_limit_bytes=58 * 2**20
        ),
    )(
        frames.T,
        counts,
        layer_norm_gain1,
        norm_gain2,
        w_in,
        w_out.T,
        w_adapt,
        grad_out,
    )
    results = pl.pallas_call(
        hand_over,
        out_shape=shapes,
        in_specs=[far] * 7,
        out_specs=[far] * 7,
        scratch_shapes=[pltpu.VMEM(one.shape, one.dtype) for one in shapes] + [pltpu.SemaphoreType.DMA((2, 7))],
        compiler_params=pltpu.CompilerParams(vmem_limit_bytes=58 * 2**20),
    )(*results)
    adapted, fg, gin, gout, *others = results
    return (adapted, fg.T, gin, gout.T, *others)


def solution(mesh):
    return jax.shard_map(
        on_device,
        mesh=mesh,
        in_specs=(
            P("dp", "tensor"),
            P("dp"),
            P(),
            P("dp", "tensor"),
            P("tensor", "dp"),
            P(),
            P("dp", "tensor"),
            P("dp", "tensor"),
        ),
        out_specs=(
            P("dp", "tensor"),
            P("dp", "tensor"),
            P("dp", "tensor"),
            P("tensor", "dp"),
            P("dp", "tensor"),
            P(),
            P(),
        ),
        check_vma=False,
    )
```

```python
import functools

import jax
import jax.numpy as jnp
from jax import lax
from jax.experimental import pallas as pl
from jax.experimental.pallas import tpu as pltpu
from jax.sharding import PartitionSpec as P

EPS = 1e-05
BF = jnp.bfloat16
F32 = jnp.float32
MESH = pl.DeviceIdType.MESH
LANES = 113


def wrap(value, size):
    return lax.rem(value + size, size)


class Place:
    def __init__(self):
        d, t = lax.axis_index("dp"), lax.axis_index("tensor")
        self.t = t
        self.at = {"x": d // 4, "z": d % 4, "y": t // 2, "c": t % 2}

    def shifted(self, axis, delta):
        return wrap(self.at[axis] + delta, 2 if axis == "c" else 4)

    def peer(self, axis, delta):
        if axis == "t":
            return {"tensor": wrap(self.t + delta, 8)}
        place = dict(self.at)
        place[axis] = self.shifted(axis, delta)
        if axis in ("x", "z"):
            return {"dp": place["x"] * 4 + place["z"]}
        return {"tensor": place["y"] * 2 + place["c"]}


class Net:
    def __init__(self, place, sems):
        self.place, self.sems = place, sems
        self.lanes = 0
        self.sent = []

    def lane(self):
        self.lanes += 1
        return self.lanes - 1

    def out_lane(self, gauge):
        lane = self.lane()
        self.sent.append((lane, gauge))
        return lane

    def copy(self, src, dst, axis, delta, out, into):
        pltpu.make_async_remote_copy(
            src_ref=src,
            dst_ref=dst,
            send_sem=self.sems.at[out],
            recv_sem=self.sems.at[into],
            device_id=self.place.peer(axis, delta),
            device_id_type=MESH,
        ).start()

    def whole(self, lane, gauge):
        return pltpu.make_async_remote_copy(
            src_ref=gauge,
            dst_ref=gauge,
            send_sem=self.sems.at[lane],
            recv_sem=self.sems.at[lane],
            device_id=self.place.peer("c", 1),
            device_id_type=MESH,
        )

    def arrived(self, lane, gauge):
        self.whole(lane, gauge).wait_recv()

    def drain(self):
        for lane, gauge in self.sent:
            self.whole(lane, gauge).wait_send()


LOW, HIGH, ALL = pl.ds(0, 48), pl.ds(48, 48), slice(None)
HALVES = (slice(0, 16), slice(16, 32))


class Gather:
    def __init__(self, net, src, buf, half, first, own):
        self.net, self.src, self.buf, self.half, self.own = net, src, buf, half, own
        self.first, self.second = (first, "z" if first == "x" else "x")
        place = net.place
        self.p, self.q = place.at[self.first], place.at[self.second]
        self.out = net.out_lane(buf.at[half, pl.ds(0, 15)])
        self.near, self.far, self.last = net.lane(), net.lane(), net.lane()
        self.waves = [net.lane() for _ in range(3)]

    def slot(self, i, j, rows=ALL):
        return self.buf.at[self.half, i * 4 + j if self.first == "x" else j * 4 + i, rows]

    def wait(self, lane, blocks):
        self.net.arrived(lane, self.buf.at[self.half, pl.ds(0, blocks)])

    def both(self, src, dst, axis, lane):
        for delta in (1, -1):
            self.net.copy(src, dst, axis, delta, self.out, lane)

    def relay(self, slot, axis, lane):
        left, right = self.net.place.shifted(axis, -1), self.net.place.shifted(axis, 1)
        self.net.copy(slot(left, LOW), slot(left, LOW), axis, 1, self.out, lane)
        self.net.copy(slot(right, HIGH), slot(right, HIGH), axis, -1, self.out, lane)

    def ahead(self, delta):
        return self.net.place.shifted(self.first, delta)

    def wave(self, i, lane):
        block = self.slot(i, self.q)
        self.both(block, block, self.second, lane)

    def start(self):
        self.both(self.src, self.slot(self.p, self.q), self.first, self.near)

    def start_across(self):
        self.both(self.src, self.slot(self.p, self.q), self.second, self.waves[0])

    def pass_on(self):
        self.wait(self.near, 2)
        self.relay(lambda i, rows: self.slot(i, self.q, rows), self.first, self.far)
        self.wave(self.ahead(-1), self.waves[1])
        self.wave(self.ahead(1), self.waves[1])

    def turn(self):
        self.wait(self.far, 1)
        self.wave(self.ahead(2), self.waves[2])

    def across(self, i):
        self.relay(lambda j, rows: self.slot(i, j, rows), self.second, self.last)

    def across_own(self):
        self.wait(self.waves[0], 2)
        self.across(self.p)

    def across_next(self):
        self.wait(self.waves[1], 4)
        self.across(self.ahead(-1))
        self.across(self.ahead(1))

    def across_far(self):
        self.wait(self.waves[2], 2)
        self.across(self.ahead(2))

    def finish(self):
        self.wait(self.last, 4)
        self.own.wait()


class Scatter:
    def __init__(self, net, buf, half, first, bufs, gauge, out, out_cols):
        self.net, self.buf, self.half = net, buf, half
        self.first, self.second = (first, "z" if first == "x" else "x")
        self.hop, self.near, self.total, self.last = bufs
        self.out, self.out_cols = out, out_cols
        self.sends = net.out_lane(gauge.at[half, pl.ds(0, 15)])
        self.lanes = [net.lane() for _ in range(3)]

    def group(self, i, rows=ALL):
        if self.first == "x":
            return self.buf.at[self.half, i, :, rows]
        return self.buf.at[self.half, :, i, rows]

    def hop_at(self, side):
        return self.hop.at[self.half, side]

    def near_at(self, side, rows=ALL):
        return self.near.at[self.half, side, :, rows]

    def start(self):
        far, right, left = (self.net.place.shifted(self.first, delta) for delta in (2, 1, -1))
        for part, into, delta, lane in (
            (self.group(far, LOW), self.hop_at(0), 1, 0),
            (self.group(far, HIGH), self.hop_at(1), -1, 0),
            (self.group(right, HIGH), self.near_at(0, HIGH), 1, 1),
            (self.group(left, LOW), self.near_at(1, LOW), -1, 1),
        ):
            self.net.copy(part, into, self.first, delta, self.sends, self.lanes[lane])

    def pass_on(self):
        self.net.arrived(self.lanes[0], self.hop.at[self.half])
        right, left = self.net.place.shifted(self.first, 1), self.net.place.shifted(self.first, -1)
        for side, part, rows, delta in (
            (0, self.group(right, LOW), LOW, 1),
            (1, self.group(left, HIGH), HIGH, -1),
        ):
            part[...] = (part[...].astype(F32) + self.hop_at(side)[...].astype(F32)).astype(BF)
            self.net.copy(part, self.near_at(side, rows), self.first, delta, self.sends, self.lanes[1])

    def turn(self):
        self.net.arrived(self.lanes[1], self.near.at[self.half])
        mine = self.group(self.net.place.at[self.first])
        total = mine[...].astype(F32) + self.near_at(0)[...].astype(F32) + self.near_at(1)[...].astype(F32)
        self.total[self.half] = total.astype(BF)
        for place, delta in enumerate((2, 1, -1)):
            part = self.total.at[self.half, self.net.place.shifted(self.second, delta)]
            self.net.copy(part, self.last.at[self.half, place], self.second, delta, self.sends, self.lanes[2])

    def finish(self):
        self.net.arrived(self.lanes[2], self.last.at[self.half])
        total = self.total[self.half, self.net.place.at[self.second]].astype(F32)
        for place in range(3):
            total = total + self.last[self.half, place].astype(F32)
        self.out[:, self.out_cols] = total


class RowGather:
    def __init__(self, net, buf, rows):
        self.net, self.buf, self.rows = net, buf, rows
        self.c = net.place.at["c"]
        self.out = net.out_lane(self.slots(7))
        self.near, self.far, self.side = net.lane(), net.lane(), net.lane()

    def slots(self, count):
        return self.buf.at[pl.ds(0, count), self.rows]

    def slot(self, delta):
        return self.buf.at[self.net.place.shifted("y", delta) * 2 + self.c, self.rows]

    def beside(self, delta):
        self.net.copy(self.slot(delta), self.slot(delta), "c", 1, self.out, self.side)

    def start(self):
        for delta in (2, 1, -1):
            lane = self.far if delta == 2 else self.near
            self.net.copy(self.slot(0), self.slot(0), "y", delta, self.out, lane)
        self.beside(0)

    def pass_on(self):
        self.net.arrived(self.far, self.slot(2))
        self.beside(2)
        self.net.arrived(self.near, self.slots(2))
        self.beside(-1)
        self.beside(1)

    def finish(self):
        self.net.arrived(self.side, self.slots(4))


class RowScatter:
    def __init__(self, net, bufs):
        self.net = net
        self.part, self.side, self.sums, self.near = bufs
        self.y, self.c = net.place.at["y"], net.place.at["c"]
        self.beside, self.out = net.out_lane(self.side), net.out_lane(self.sums)
        self.one, self.two = net.lane(), [net.lane() for _ in range(2)]

    def put(self, i, value):
        self.part[i] = value.reshape(4, 2, 32, 384)
        self.net.copy(self.part.at[i, :, 1 - self.c], self.side.at[i], "c", 1, self.beside, self.one)

    def pair(self, piece, row):
        rows = HALVES[piece]
        return [self.part[i, row, self.c, rows] + self.side[i, row, rows] for i in range(4)]

    def pass_on(self):
        net = self.net
        net.arrived(self.one, self.side)
        for piece in range(2):
            for place, delta in enumerate((2, 1, -1)):
                for i, value in enumerate(self.pair(piece, net.place.shifted("y", delta))):
                    self.sums[piece, place, :, i * 384 : (i + 1) * 384] = value.astype(BF)
                net.copy(
                    self.sums.at[piece, place], self.near.at[piece, place], "y", delta, self.out, self.two[piece]
                )

    def finish(self, piece):
        total = jnp.concatenate(self.pair(piece, self.y), axis=1)
        self.net.arrived(self.two[piece], self.near.at[piece])
        for place in range(3):
            total = total + self.near[piece, place].astype(F32)
        return total


def row_norm(values):
    center = values - jnp.mean(values, axis=-1, keepdims=True)
    scale = lax.rsqrt(jnp.mean(center * center, axis=-1, keepdims=True) + EPS)
    return (center * scale, scale)


def row_norm_gradient(d_hat, vhat, scale):
    first = jnp.mean(d_hat, axis=-1, keepdims=True)
    second = jnp.mean(d_hat * vhat, axis=-1, keepdims=True)
    return scale * (d_hat - first - vhat * second)


def times(left, right):
    return jnp.dot(left, right, preferred_element_type=F32)


def times_t(left, right):
    return lax.dot_general(left, right, (((1,), (1,)), ((), ())), preferred_element_type=F32)


def kernel(
    frames_in, counts_in, gain1_in, gain2_in, w_in, w_out, w_ad, grad_out,
    adapted_h, fg_h, gin_h, gout_h, gad_h, gain1_h, gain2_h,
    wi, wo, wa, gi, go, ga,
    hop_i, near_i, tot_i, last_i,
    hop_o, near_o, tot_o, last_o,
    hop_a, near_a, tot_a, last_a,
    adapted_o, fg_o, gin_o, gout_o, gad_o, gain1_o, gain2_o,
    counts, frames, gain1_v, gain2_v, own,
    fr, rows, hid, nrm, dbr, hid_t, nrm_t, dbr_t,
    part_b, side_b, sums_b, near_b,
    part_n, side_n, sums_n, near_n,
    part_h, side_h, sums_h, near_h,
    xhat, yhat, dres, cot, factor, swished, fgs, fgr,
    gn_c, gn_y, gn_x, gn_z,
    sems, local,
):
    place = Place()
    net = Net(place, sems)
    x, z, y, c, t = place.at["x"], place.at["z"], place.at["y"], place.at["c"], place.t

    greeted = [("t", delta) for delta in range(1, 8)] + [(a, delta) for a in "xz" for delta in (1, -1, 2)]
    barrier = pltpu.get_barrier_semaphore()
    for axis, delta in greeted:
        pl.semaphore_signal(barrier, inc=1, device_id=place.peer(axis, delta), device_id_type=MESH)

    loads = []

    def load(src, dst):
        move = pltpu.make_async_copy(src, dst, local.at[len(loads)])
        move.start()
        loads.append(move)
        return move

    frames_load = load(frames_in, frames)
    gain_loads = [load(gain1_in, gain1_v), load(gain2_in, gain2_v)]
    gathers = []
    for src, buf, width in ((w_in, wi, 256), (w_out, wo, 256), (w_ad, wa, 512)):
        for half in range(2):
            cut = src.at[:, pl.ds(half * width, width)]
            gathers.append(Gather(net, cut, buf, half, "xz"[half], load(cut, buf.at[half, x * 4 + z])))
    i0, i1, o0, o1, a0, a1 = gathers
    cot_load = load(grad_out, cot)
    counts_load = load(counts_in, counts)
    frames_load.wait()
    own[...] = frames[...].T.reshape(8, 32, 192)
    pl.semaphore_wait(barrier, len(greeted))

    def to_peers(src, dst, out, into):
        for delta in range(1, 8):
            net.copy(src.at[wrap(t + delta, 8)], dst.at[t], "t", delta, out, into)

    frames_lane = net.lane()
    to_peers(own, fr, net.out_lane(own.at[pl.ds(0, 7)]), frames_lane)
    for one in (i0, i1):
        one.start()
        one.start_across()
    o0.start()
    o1.start()
    cot_load.wait()
    counts_load.wait()
    live = lax.broadcasted_iota(jnp.int32, (256, 1), 0) < counts[0]
    cot[...] = jnp.where(live, cot[...].astype(F32), 0.0).astype(BF)

    fr[t] = own[t]
    for one in gain_loads:
        one.wait()
    gain1, gain2 = gain1_v[...].reshape(1, 1536), gain2_v[...].reshape(1, 1536)
    net.arrived(frames_lane, fr.at[pl.ds(0, 7)])
    for piece in range(8):
        rows[:, piece * 192 : (piece + 1) * 192] = fr[piece].astype(F32)
    normal, rstd1 = row_norm(rows[...])
    xhat[...] = normal
    hid[t] = (normal * gain1).astype(BF)
    hid_rows = RowGather(net, hid, slice(0, 32))
    hid_rows.start()

    i0.pass_on()
    i0.across_own()
    i1.across_own()
    i1.pass_on()
    o0.start_across()
    o1.start_across()
    o0.pass_on()
    o1.pass_on()
    i0.turn()
    i0.across_next()
    i1.turn()
    i1.across_next()
    hid_rows.pass_on()
    o0.across_own()
    o1.across_own()
    o0.turn()
    hid_rows.finish()

    def flat(ref):
        return ref[...].reshape(256, 1536)

    hid_t[...] = flat(hid).T
    o0.across_next()
    o1.turn()
    o1.across_next()
    i0.across_far()
    i1.across_far()
    o0.across_far()
    o1.across_far()
    a1.start()
    a0.start()
    a1.start_across()

    def front(half):
        pre = times(flat(hid), wi[half].reshape(1536, 256))
        sig = jax.nn.sigmoid(pre)
        swished[half] = (pre * sig).astype(BF)
        factor[half] = sig * (1.0 + pre * (1.0 - sig))

    i0.finish()
    front(0)
    i1.finish()
    front(1)
    a0.start_across()
    o0.finish()
    o1.finish()

    def rows_out(scatter, left, weight, look=None):
        for i in range(4):
            some = slice(4 * i, 4 * i + 4)
            value = times_t(left(0), weight[0, some].reshape(384, -1))
            value = value + times_t(left(1), weight[1, some].reshape(384, -1))
            scatter.put(i, value)
            if look is not None:
                look(i, value)

    branch = RowScatter(net, (part_b, side_b, sums_b, near_b))
    rows_out(branch, lambda half: swished[half], wo)
    branch.pass_on()
    a1.pass_on()
    a0.pass_on()
    a0.across_own()
    a1.across_own()

    rstd2 = []
    nrm_rows = [RowGather(net, nrm, piece) for piece in HALVES]

    def middle(piece):
        half = HALVES[piece]
        normal, scale = row_norm(rows[half] + 0.5 * branch.finish(piece))
        rstd2.append(scale)
        yhat[half] = normal
        nrm[t, half] = (normal * gain2).astype(BF)
        nrm_rows[piece].start()

    middle(0)
    a1.turn()
    middle(1)
    a0.turn()
    a1.across_next()
    nrm_rows[0].pass_on()
    a0.across_next()
    nrm_rows[1].pass_on()
    a1.across_far()
    a0.across_far()
    nrm_rows[0].finish()
    nrm_rows[1].finish()

    def outer(grad, half, left, right):
        def body(i, carry):
            some = left[pl.ds(pl.multiple_of(i * 384, 128), 384), :]
            grad[half, i] = times(some, right).astype(BF).reshape(4, 96, -1)
            return carry

        lax.fori_loop(0, 4, body, 0)

    def scatter(buf, bufs, gauge, out, width):
        return [
            Scatter(net, buf, half, "zx"[half], bufs, gauge, out, pl.ds(half * width, width))
            for half in range(2)
        ]

    sa0, sa1 = scatter(ga, (hop_a, near_a, tot_a, last_a), wa, gad_o, 512)
    so0, so1 = scatter(go, (hop_o, near_o, tot_o, last_o), wo, gout_o, 256)
    si0, si1 = scatter(gi, (hop_i, near_i, tot_i, last_i), wi, gin_o, 256)

    nrm_t[...] = flat(nrm).T
    outer(ga, 0, nrm_t, cot[:, :512])
    sa0.start()
    outer(ga, 1, nrm_t, cot[:, 512:])
    sa1.start()

    a0.finish()
    a1.finish()
    d_norm = RowScatter(net, (part_n, side_n, sums_n, near_n))
    rows_out(d_norm, lambda half: cot[:, half * 512 : (half + 1) * 512], wa)

    def adapt(half):
        value = times(flat(nrm), wa[half].reshape(1536, 512))
        adapted_o[:, half * 512 : (half + 1) * 512] = jnp.where(live, value, 0.0).astype(BF)

    adapt(0)
    d_norm.pass_on()
    adapt(1)
    stores = [load(adapted_o, adapted_h)]
    sa0.pass_on()
    sa1.pass_on()

    gain2_parts = []
    dbr_rows = [RowGather(net, dbr, piece) for piece in HALVES]

    def back(piece):
        half = HALVES[piece]
        d_normed, normal = d_norm.finish(piece), yhat[half]
        gain2_parts.append(jnp.sum(d_normed * normal, axis=0, keepdims=True))
        d_resid = row_norm_gradient(d_normed * gain2, normal, rstd2[piece])
        dres[half] = d_resid
        dbr[t, half] = (0.5 * d_resid).astype(BF)
        dbr_rows[piece].start()

    back(0)
    back(1)
    dbr_rows[0].pass_on()
    sa0.turn()
    dbr_rows[0].finish()
    dbr_rows[1].pass_on()
    sa1.turn()
    dbr_rows[1].finish()

    pres = []

    def before(half):
        d_swished = times(flat(dbr), wo[half].reshape(1536, 256))
        pres.append((d_swished * factor[half]).astype(BF))

    def gain_start(buf, axis, total):
        here = buf.at[place.at[axis]]
        here[...] = total
        out, into = net.out_lane(buf.at[pl.ds(0, 3)]), net.lane()
        for delta in (1, -1, 2):
            net.copy(here, here, axis, delta, out, into)
        return into

    def gain_sum(into, buf):
        net.arrived(into, buf.at[pl.ds(0, 3)])
        return buf[0] + buf[1] + buf[2] + buf[3]

    dbr_t[...] = flat(dbr).T
    outer(go, 0, dbr_t, swished[0])
    so0.start()
    outer(go, 1, dbr_t, swished[1])
    so1.start()
    before(0)
    before(1)
    d_hid = RowScatter(net, (part_h, side_h, sums_h, near_h))
    gain1_sums = []

    def look(i, value):
        some = hid[:, :, i * 384 : (i + 1) * 384].reshape(256, 384).astype(F32)
        gain1_sums.append(jnp.sum(value * some, axis=0, keepdims=True))

    rows_out(d_hid, lambda half: pres[half], wi, look)
    gain1_part = jnp.concatenate(gain1_sums, axis=1) / gain1
    gn_c[c] = jnp.concatenate([gain1_part, gain2_parts[0] + gain2_parts[1]], axis=0)
    lane = net.lane()
    net.copy(gn_c.at[c], gn_c.at[c], "c", 1, net.out_lane(gn_c.at[0]), lane)

    outer(gi, 0, hid_t, pres[0])
    si0.start()
    d_hid.pass_on()
    outer(gi, 1, hid_t, pres[1])
    si1.start()
    net.arrived(lane, gn_c.at[1 - c])
    lane = gain_start(gn_y, "y", gn_c[0] + gn_c[1])
    so0.pass_on()
    so1.pass_on()
    lane = gain_start(gn_x, "x", gain_sum(lane, gn_y))
    si0.pass_on()
    si1.pass_on()

    d_hidden = jnp.concatenate([d_hid.finish(0), d_hid.finish(1)], axis=0)
    grad_rows = dres[...] + row_norm_gradient(d_hidden * gain1, xhat[...], rstd1)
    for piece in range(8):
        fgs[piece] = grad_rows[:, piece * 192 : (piece + 1) * 192]
    fgr[t] = fgs[t]
    rows_lane = net.lane()
    to_peers(fgs, fgr, net.out_lane(fgs.at[pl.ds(0, 7)]), rows_lane)
    sa1.finish()
    sa0.finish()
    stores.append(load(gad_o, gad_h))
    lane = gain_start(gn_z, "z", gain_sum(lane, gn_x))
    so0.turn()
    so1.turn()
    net.arrived(rows_lane, fgr.at[pl.ds(0, 7)])
    fg_o[...] = fgr[...].reshape(256, 192).T
    stores.append(load(fg_o, fg_h))
    si0.turn()
    si1.turn()
    total = gain_sum(lane, gn_z)
    gain1_o[...] = total[0]
    gain2_o[...] = total[1]
    stores.append(load(gain1_o, gain1_h))
    stores.append(load(gain2_o, gain2_h))
    so0.finish()
    so1.finish()
    stores.append(load(gout_o, gout_h))
    si0.finish()
    si1.finish()
    stores.append(load(gin_o, gin_h))
    net.drain()
    for move in stores:
        move.wait()


def hand_over(*refs):
    count = len(refs) // 3
    sems = refs[-1]
    moves = []
    for i in range(count):
        hold = refs[2 * count + i]
        moves.append(
            (
                pltpu.make_async_copy(refs[i], hold, sems.at[0, i]),
                pltpu.make_async_copy(hold, refs[count + i], sems.at[1, i]),
            )
        )
        moves[-1][0].start()
    for come, go in moves:
        come.wait()
        go.start()
    for come, go in moves:
        go.wait()


def on_device(frames, counts, layer_norm_gain1, w_in, w_out, norm_gain2, w_adapt, grad_out):
    def weight(width):
        return pltpu.VMEM((2, 16, 96, width), BF)

    def gradient(width):
        return pltpu.VMEM((2, 4, 4, 96, width), BF)

    def sums(width):
        return [
            pltpu.VMEM((2, 2, 4, 48, width), BF),
            pltpu.VMEM((2, 2, 4, 96, width), BF),
            pltpu.VMEM((2, 4, 96, width), BF),
            pltpu.VMEM((2, 3, 96, width), BF),
        ]

    shape = jax.ShapeDtypeStruct
    shapes = (
        shape((256, 1024), BF),
        shape((192, 256), F32),
        shape((96, 512), F32),
        shape((96, 512), F32),
        shape((96, 1024), F32),
        shape((1536,), F32),
        shape((1536,), F32),
    )
    slots = pltpu.VMEM((8, 32, 1536), BF)
    row_sums = [
        pltpu.VMEM((4, 4, 2, 32, 384), F32),
        pltpu.VMEM((4, 4, 32, 384), F32),
        pltpu.VMEM((2, 3, 16, 1536), BF),
        pltpu.VMEM((2, 3, 16, 1536), BF),
    ]
    scratch = (
        [weight(256), weight(256), weight(512), gradient(256), gradient(256), gradient(512)]
        + sums(256)
        + sums(256)
        + sums(512)
        + [pltpu.VMEM(one.shape, one.dtype) for one in shapes]
        + [pltpu.SMEM((1,), jnp.int32), pltpu.VMEM((192, 256), BF), pltpu.VMEM((1536,), F32), pltpu.VMEM((1536,), F32)]
        + [pltpu.VMEM((8, 32, 192), BF)]
        + [pltpu.VMEM((8, 32, 192), BF), pltpu.VMEM((32, 1536), F32)]
        + [slots] * 3
        + [pltpu.VMEM((1536, 256), BF)] * 3
        + row_sums * 3
        + [pltpu.VMEM((32, 1536), F32)] * 3
        + [pltpu.VMEM((256, 1024), BF)]
        + [pltpu.VMEM((2, 256, 256), F32), pltpu.VMEM((2, 256, 256), BF)]
        + [pltpu.VMEM((8, 32, 192), F32)] * 2
        + [pltpu.VMEM((2, 2, 1536), F32)]
        + [pltpu.VMEM((4, 2, 1536), F32)] * 3
        + [pltpu.SemaphoreType.DMA((LANES,)), pltpu.SemaphoreType.DMA((18,))]
    )
    far = pl.BlockSpec(memory_space=pl.ANY)
    results = pl.pallas_call(
        kernel,
        out_shape=shapes,
        in_specs=[far] * 8,
        out_specs=[far] * 7,
        scratch_shapes=scratch,
        compiler_params=pltpu.CompilerParams(
            collective_id=0, has_side_effects=True, vmem_limit_bytes=58 * 2**20
        ),
    )(
        frames.T,
        counts,
        layer_norm_gain1,
        norm_gain2,
        w_in,
        w_out.T,
        w_adapt,
        grad_out,
    )
    results = pl.pallas_call(
        hand_over,
        out_shape=shapes,
        in_specs=[far] * 7,
        out_specs=[far] * 7,
        scratch_shapes=[pltpu.VMEM(one.shape, one.dtype) for one in shapes] + [pltpu.SemaphoreType.DMA((2, 7))],
        compiler_params=pltpu.CompilerParams(vmem_limit_bytes=58 * 2**20),
    )(*results)
    adapted, fg, gin, gout, *others = results
    return (adapted, fg.T, gin, gout.T, *others)


def solution(mesh):
    return jax.shard_map(
        on_device,
        mesh=mesh,
        in_specs=(
            P("dp", "tensor"),
            P("dp"),
            P(),
            P("dp", "tensor"),
            P("tensor", "dp"),
            P(),
            P("dp", "tensor"),
            P("dp", "tensor"),
        ),
        out_specs=(
            P("dp", "tensor"),
            P("dp", "tensor"),
            P("dp", "tensor"),
            P("tensor", "dp"),
            P("dp", "tensor"),
            P(),
            P(),
        ),
        check_vma=False,
    )
```
